128 devices in a mesh: ctx: 16 (over z_hi, y, core), heads: 8 (over z_lo, x).
Axes of the slice: x: 4, y: 4, z: 4 (z_hi: 2, z_lo: 2; z = z_hi * 2 + z_lo), core: 2. Of those that a mesh axis runs over, the one named last changes fastest.
Arguments:
- stretch_order: int32 [32], replicated, may hold values from 0 to 31, as said below
- query_heads: bfloat16 [2048, 4096], P('ctx', 'heads'), may hold values from -5 to 5
- key_heads: bfloat16 [2048, 4096], P('ctx', 'heads'), may hold values from -5 to 5
- value_heads: bfloat16 [2048, 4096], P('ctx', 'heads'), may hold values from -6 to 6
- output_grad: bfloat16 [2048, 4096], P('ctx', 'heads'), may hold values from -6 to 6
- query_weight: bfloat16 [4096, 4096], P(None, 'heads'), may hold values from -0.09375 to 0.09375
- key_weight: bfloat16 [4096, 4096], P(None, 'heads'), may hold values from -0.09375 to 0.09375
- value_weight: bfloat16 [4096, 4096], P(None, 'heads'), may hold values from -0.09375 to 0.09375
- output_weight: bfloat16 [4096, 4096], P('heads'), may hold values from -0.09375 to 0.09375
- head_lambda: float32 [16], P('heads'), may hold values from 0.2 to 0.8
- norm_gain: float32 [256], replicated, may hold values from 0.1 to 1.9
Outputs:
- input_grad: float32 [4096, 2048], P('heads', 'ctx')
The draws below stay inside these ranges and needn't reach their ends.
Inputs may be any that keep to these rules, and one draw needn't show every extreme that they name: `stretch_order`: every stretch 0 to 31 appears once; entries 2 d and 2 d + 1 always sum to 31.
All inputs are finite; a program needn't handle non-finite values.
Results may differ from the reference program's by a relative error of at most 0.024.
Values may be sent and summed in bfloat16 or wider, within the bound.
A program may use at most 128 MiB of HBM per device.

```python
import jax
import jax.numpy as jnp
from jax import lax

D = 4096
HEADS = 16
HDIM = 128
INNER = 4096
TOKENS = 2048
STRETCH = 64
NCHUNK = 32


def draw_stretch_order(key, part):
    key = jax.random.fold_in(key, 7)
    pairs = jax.random.permutation(jax.random.fold_in(key, 1), NCHUNK // 2).astype(jnp.int32)
    flips = jax.random.randint(jax.random.fold_in(key, 2), (NCHUNK // 2,), 0, 2)
    first_stretch = jnp.where(flips == 1, NCHUNK - 1 - pairs, pairs)
    return jnp.stack([first_stretch, NCHUNK - 1 - first_stretch], axis=1).reshape(NCHUNK).astype(jnp.int32)


def draw_query_heads(key, part):
    own_key = jax.random.fold_in(key, 3)
    result = jax.random.truncated_normal(own_key, -4.0, 4.0, (TOKENS, INNER), jnp.float32)
    return result.astype(jnp.bfloat16)


def draw_key_heads(key, part):
    own_key = jax.random.fold_in(key, 5)
    result = jax.random.truncated_normal(own_key, -4.0, 4.0, (TOKENS, INNER), jnp.float32)
    return result.astype(jnp.bfloat16)


def block_scale(rng, dims, pieces, least, largest):
    def one(axis_at, parts):
        steps = jax.random.uniform(jax.random.fold_in(jax.random.fold_in(rng, 6), axis_at), (parts,), jnp.float32, least / len(pieces), largest / len(pieces))
        return jnp.repeat(jnp.exp(steps), dims[axis_at] // parts).reshape((-1,) + (1,) * (len(dims) - axis_at - 1))

    gain = one(*pieces[0])
    for cut in pieces[1:]:
        gain = gain * one(*cut)
    return gain


def centred(key, extent, spread, limit, shards=(), held_as=jnp.bfloat16):
    entries = spread * jax.random.normal(key, extent, jnp.float32)
    if shards:
        entries = entries * block_scale(key, extent, shards, -0.22, 0.18)
    return jnp.clip(entries, -limit, limit).astype(held_as)


def setup_inputs(seed: int = 0) -> dict:
    streams_of = jax.random.split(jax.random.key(seed), 12)
    return {
        "stretch_order": draw_stretch_order(jax.random.fold_in(streams_of[11], 71), 0),
        "query_heads": draw_query_heads(jax.random.fold_in(streams_of[11], 71), 0),
        "key_heads": draw_key_heads(jax.random.fold_in(streams_of[11], 71), 0),
        "value_heads": centred(streams_of[3], (TOKENS, INNER), 1.0, 6.0, ((0, 16), (1, 8))),
        "output_grad": centred(streams_of[4], (TOKENS, D), 1.0, 6.0, ((0, 16), (1, 8))),
        "query_weight": centred(streams_of[5], (D, INNER), D ** -0.5, 0.09375, ((1, 8),)),
        "key_weight": centred(streams_of[6], (D, INNER), D ** -0.5, 0.09375, ((1, 8),)),
        "value_weight": centred(streams_of[7], (D, INNER), D ** -0.5, 0.09375, ((1, 8),)),
        "output_weight": centred(streams_of[8], (INNER, D), INNER ** -0.5, 0.09375, ((0, 8),)),
        "head_lambda": jnp.clip(0.2 + 0.6 * jax.random.uniform(streams_of[9], (HEADS,), jnp.float32) ** block_scale(streams_of[9], (HEADS,), ((0, 8),), -0.2, 0.2), 0.2, 0.8),
        "norm_gain": jnp.clip(1.0 + 0.18 * jax.random.normal(streams_of[10], (2 * HDIM,), jnp.float32), 0.1, 1.9),
    }


lambda_init = 0.8
norm_epsilon = 1e-05

def token_positions(stretch_order):
    row_index = jnp.arange(TOKENS, dtype=jnp.int32)
    return jnp.take(stretch_order, row_index // STRETCH) * STRETCH + row_index % STRETCH

def head_gradients(head_index, query_heads, key_heads, value_heads, out_heads, head_lambda, norm_gain, visible):
    head_width = 2 * HDIM
    offset = head_index * head_width
    query_head = lax.dynamic_slice_in_dim(query_heads, offset, head_width, 1)
    key_head = lax.dynamic_slice_in_dim(key_heads, offset, head_width, 1)
    value_head = lax.dynamic_slice_in_dim(value_heads, offset, head_width, 1)
    grad_head = lax.dynamic_slice_in_dim(out_heads, offset, head_width, 1)
    weight = head_lambda[head_index]
    score_scale = HDIM ** (-0.5)
    probabilities = []
    for half_index in range(2):
        query_half = query_head[:, half_index * HDIM:(half_index + 1) * HDIM]
        key_half = key_head[:, half_index * HDIM:(half_index + 1) * HDIM]
        scores = jnp.dot(query_half, key_half.T, preferred_element_type=jnp.float32) * score_scale
        scores = jnp.where(visible, scores, -jnp.inf)
        row_peak = lax.optimization_barrier(jnp.max(scores, axis=1, keepdims=True))
        log_total = row_peak + jnp.log(lax.optimization_barrier(jnp.sum(jnp.exp(scores - row_peak), axis=1, keepdims=True)))
        probabilities.append(jnp.exp(scores - log_total))
    first_out = jnp.dot(probabilities[0].astype(jnp.bfloat16), value_head, preferred_element_type=jnp.float32)
    second_out = jnp.dot(probabilities[1].astype(jnp.bfloat16), value_head, preferred_element_type=jnp.float32)
    combined = first_out - weight * second_out
    root_mean = jnp.sqrt(lax.optimization_barrier(jnp.mean(combined * combined, axis=1, keepdims=True)) + norm_epsilon)
    normed = combined / root_mean
    grad_normed = grad_head * norm_gain * (1.0 - lambda_init)
    grad_attn = ((grad_normed - normed * lax.optimization_barrier(jnp.mean(grad_normed * normed, axis=1, keepdims=True))) / root_mean).astype(jnp.bfloat16)
    grad_float = grad_attn.astype(jnp.float32)
    first_stat = lax.optimization_barrier(jnp.sum(grad_float * first_out, axis=1, keepdims=True))
    second_stat = lax.optimization_barrier(jnp.sum(grad_float * second_out, axis=1, keepdims=True))
    grad_weights = jnp.dot(grad_attn, value_head.T, preferred_element_type=jnp.float32)
    first_grad = (probabilities[0] * (grad_weights - first_stat)).astype(jnp.bfloat16)
    second_grad = (-weight * probabilities[1] * (grad_weights - second_stat)).astype(jnp.bfloat16)
    mixed_weights = (probabilities[0] - weight * probabilities[1]).astype(jnp.bfloat16)
    value_grad = jnp.dot(mixed_weights.T, grad_attn, preferred_element_type=jnp.float32)
    query_grad = jnp.concatenate([score_scale * jnp.dot(first_grad, key_head[:, :HDIM], preferred_element_type=jnp.float32), score_scale * jnp.dot(second_grad, key_head[:, HDIM:], preferred_element_type=jnp.float32)], axis=1)
    key_grad = jnp.concatenate([score_scale * jnp.dot(first_grad.T, query_head[:, :HDIM], preferred_element_type=jnp.float32), score_scale * jnp.dot(second_grad.T, query_head[:, HDIM:], preferred_element_type=jnp.float32)], axis=1)
    return (query_grad.astype(jnp.bfloat16), key_grad.astype(jnp.bfloat16), value_grad.astype(jnp.bfloat16))

def reference(stretch_order, query_heads, key_heads, value_heads, output_grad, query_weight, key_weight, value_weight, output_weight, head_lambda, norm_gain):
    positions = token_positions(stretch_order)
    visible = positions[None, :] <= positions[:, None]
    out_heads = jnp.dot(output_grad, output_weight.T, preferred_element_type=jnp.float32)

    def one_head(head_index):
        return head_gradients(head_index, query_heads, key_heads, value_heads, out_heads, head_lambda, norm_gain, visible)
    query_grads, key_grads, value_grads = lax.map(one_head, jnp.arange(HEADS, dtype=jnp.int32))

    def flatten(stacked):
        return jnp.transpose(stacked, (1, 0, 2)).reshape(TOKENS, INNER)
    summed = jnp.dot(query_weight, flatten(query_grads).T, preferred_element_type=jnp.float32)
    summed = summed + jnp.dot(key_weight, flatten(key_grads).T, preferred_element_type=jnp.float32)
    summed = summed + jnp.dot(value_weight, flatten(value_grads).T, preferred_element_type=jnp.float32)
    return summed
```

```python
import functools

import jax
import jax.numpy as jnp
from jax import lax
from jax.experimental import pallas as pl
from jax.experimental.pallas import tpu as pltpu
from jax.sharding import PartitionSpec as P

MESH = pl.DeviceIdType.MESH
HDIM = 128
WIDTH = 256
LAMBDA_INIT = 0.8
EPSILON = 1e-05
MASKED = -1e30
SCALE = HDIM**-0.5
LOG2E = 1.4426950408889634
F32 = jnp.float32
BF16 = jnp.bfloat16


def mm(a, b, dims=((1,), (0,))):
    return lax.dot_general(a, b, (dims, ((), ())), preferred_element_type=F32)


NT = ((1,), (1,))
TN = ((0,), (0,))


def kernel(
    order, lam, gain, qh, kh, vh, og, wq, wk, wv, wo, out,
    kb, vb, qb, gs, gb, ogb, wob, wb, ls, lr, st, qt, d0, ot, gacc, gt, gn, dq,
    sibs, sibr, own, ys, yr, yf, dqs, dks, rb, pa, xs_, xr, xf, zs, zr,
    wsem, lsem, ssem, rsem,
):
    ctx = lax.axis_index("ctx")
    hd = lax.axis_index("heads")
    hi = lax.div(ctx, 8)
    y = lax.rem(lax.div(ctx, 2), 4)
    c = lax.rem(ctx, 2)
    lo = lax.div(hd, 4)
    x = lax.rem(hd, 4)

    def dev(hi_, y_, c_, lo_, x_):
        return (hi_ * 8 + y_ * 2 + c_, lo_ * 4 + x_)

    sib = dev(hi, y, 1 - c, lo, x)
    yp = dev(hi, lax.rem(y + 1, 4), c, lo, x)
    ym = dev(hi, lax.rem(y + 3, 4), c, lo, x)
    xp = dev(hi, y, c, lo, lax.rem(x + 1, 4))
    xm = dev(hi, y, c, lo, lax.rem(x + 3, 4))
    zn = [dev(a, y, c, 1 - lo, x) for a in range(2)]
    partner = dev(hi, y, c, 1 - lo, x)

    local = []
    own_og = pltpu.make_async_copy(og, ogb.at[0, 0], lsem.at[0])
    own_og.start()
    wo_copies = {}
    for s in range(4):
        for r in range(2):
            block = lax.rem(lo + r, 2) * 4 + lax.rem(x + s, 4)
            at = pl.ds(pl.multiple_of(block * 512, 512), 512)
            cp = pltpu.make_async_copy(wo.at[:, at], wob.at[r, s], wsem.at[3, r, s])
            cp.start()
            wo_copies[r, s] = cp
    w_copies = {}
    for k, w in enumerate((wq, wk, wv)):
        for s in (2, 1, 3, 0):
            for r in (1, 0):
                block = lax.rem(lo + r, 2) * 4 + lax.rem(x + s, 4)
                at = pl.ds(pl.multiple_of(block * 512, 512), 512)
                cp = pltpu.make_async_copy(w.at[at, :], wb.at[k, r, s], wsem.at[k, r, s])
                cp.start()
                w_copies[k, r, s] = cp

    ls[...] = jnp.full((8, 128), lam[hi], F32)

    barrier = pltpu.get_barrier_semaphore()
    for d in (sib, yp, ym, xp, xm, zn[0], zn[1]):
        pl.semaphore_signal(barrier, inc=1, device_id=d, device_id_type=MESH)
    pl.semaphore_wait(barrier, 7)

    used = [0]
    sent = []

    def send(src, dst, recv, to):
        n = used[0]
        used[0] += 1
        cp = pltpu.make_async_remote_copy(
            src_ref=src, dst_ref=dst, send_sem=ssem.at[n], recv_sem=rsem.at[recv],
            device_id=to, device_id_type=MESH,
        )
        cp.start()
        sent.append(cp)

    def arrived(dst, recv):
        pltpu.make_async_remote_copy(
            src_ref=dst, dst_ref=dst, send_sem=ssem.at[0], recv_sem=rsem.at[recv],
            device_id=sib, device_id_type=MESH,
        ).wait_recv()

    names = {}

    def num(*key):
        if key not in names:
            names[key] = len(names)
        return names[key]

    for kind in ("k", "v", "q", "g", "dq", "dk", "dv"):
        for a in range(2):
            num("z", kind, a)

    def zsend(src, dst, kind, a):
        send(src, dst, num("z", kind, 0) + hi, zn[a])

    mine = pl.ds(pl.multiple_of(hi * 128, 128), 128)
    for a in range(2):
        zsend(kh.at[:, a * 256 : a * 256 + 256], kb.at[0, 0, mine], "k", a)
    send(og, ogb.at[0, 3], num("og", 0, 3), xp)
    send(og, ogb.at[0, 1], num("og", 0, 1), xm)
    for a in range(2):
        zsend(vh.at[:, a * 256 : a * 256 + 256], vb.at[0, 0, mine], "v", a)
    send(og, ogb.at[1, 0], num("og", 1, 0), partner)
    for a in range(2):
        zsend(qh.at[:, a * 256 : a * 256 + 256], qb.at[mine], "q", a)
    send(ls, lr, num("lam"), partner)

    def first(buf, kind):
        for a in range(2):
            arrived(buf.at[0, 0, pl.ds(a * 128, 128)], num("z", kind, a))
        send(buf.at[0, 0], buf.at[3, 0], num(kind, 3, 0), yp)
        send(buf.at[0, 0], buf.at[1, 0], num(kind, 1, 0), ym)
        send(buf.at[0, 0], buf.at[0, 1], num(kind, 0, 1), sib)

    def relay(buf, kind):
        lower, upper = pl.ds(0, 128), pl.ds(128, 128)
        arrived(buf.at[3, 0], num(kind, 3, 0))
        send(buf.at[3, 0, lower], buf.at[2, 0, lower], num(kind, 2, 0, 0), yp)
        arrived(buf.at[1, 0], num(kind, 1, 0))
        send(buf.at[1, 0, upper], buf.at[2, 0, upper], num(kind, 2, 0, 1), ym)
        send(buf.at[3, 0], buf.at[3, 1], num(kind, 3, 1), sib)
        send(buf.at[1, 0], buf.at[1, 1], num(kind, 1, 1), sib)

    def last(buf, kind):
        arrived(buf.at[2, 0, pl.ds(0, 128)], num(kind, 2, 0, 0))
        arrived(buf.at[2, 0, pl.ds(128, 128)], num(kind, 2, 0, 1))
        send(buf.at[2, 0], buf.at[2, 1], num(kind, 2, 1), sib)

    first(kb, "k")
    first(vb, "v")

    lane = lax.broadcasted_iota(jnp.int32, (64, 256), 1)
    row = lax.broadcasted_iota(jnp.int32, (64, 256), 0)

    def stretch(hi_, s, r, half):
        block = hi_ * 8 + lax.rem(y + s, 4) * 2 + lax.rem(c + r, 2)
        return order[block * 2 + half]

    qs = [stretch(h, 0, 0, half) for h in range(2) for half in range(2)]
    qstretch = jnp.where(
        lane < 128,
        jnp.where(lane < 64, qs[0], qs[1]),
        jnp.where(lane < 192, qs[2], qs[3]),
    )
    d0[...] = row - qstretch * 64 - lax.rem(lane, 64)

    own_og.wait()
    arrived(ogb.at[1, 0], num("og", 1, 0))
    send(ogb.at[1, 0], ogb.at[1, 3], num("og", 1, 3), xp)
    send(ogb.at[1, 0], ogb.at[1, 1], num("og", 1, 1), xm)

    for a in range(2):
        arrived(qb.at[pl.ds(a * 128, 128)], num("z", "q", a))
    for j in range(2):
        qt[j] = jnp.transpose(qb[:, j * 128 : j * 128 + 128].astype(F32)).astype(BF16)

    def scores(s, r, peak):
        i = s * 2 + r
        peaks = list(peak)
        for j in range(2):
            sc = mm(kb[s, r, :, j * 128 : j * 128 + 128], qt[j]) * (SCALE * LOG2E)
            for n in range(4):
                threshold = stretch(n // 2, s, r, n % 2) * -64
                part = jnp.where(d0[...] <= threshold, sc[n * 64 : n * 64 + 64], MASKED)
                st[j, i, n * 64 : n * 64 + 64] = part
                peaks[j] = jnp.maximum(peaks[j], jnp.max(part.reshape(8, 8, 256), axis=0))
        return tuple(peaks)

    def gdot(r, s, start=False):
        wo_copies[r, s].wait()
        term = mm(wob[r, s], ogb[r, s], NT)
        gacc[...] = term if start else gacc[...] + term

    peak = (jnp.full((8, 256), MASKED, F32),) * 2
    peak = scores(0, 0, peak)
    gdot(0, 0, True)
    relay(kb, "k")
    arrived(kb.at[0, 1], num("k", 0, 1))
    peak = scores(0, 1, peak)
    gdot(1, 0)
    arrived(ogb.at[0, 3], num("og", 0, 3))
    send(ogb.at[0, 3], ogb.at[0, 2], num("og", 0, 2), xp)
    relay(vb, "v")
    arrived(ogb.at[0, 1], num("og", 0, 1))
    gdot(0, 3)
    gdot(0, 1)
    peak = scores(1, 0, peak)
    peak = scores(3, 0, peak)
    arrived(kb.at[1, 1], num("k", 1, 1))
    peak = scores(1, 1, peak)
    arrived(kb.at[3, 1], num("k", 3, 1))
    peak = scores(3, 1, peak)
    arrived(ogb.at[1, 1], num("og", 1, 1))
    send(ogb.at[1, 1], ogb.at[1, 2], num("og", 1, 2), xm)
    last(kb, "k")
    arrived(ogb.at[1, 3], num("og", 1, 3))
    gdot(1, 3)
    gdot(1, 1)
    peak = scores(2, 0, peak)
    arrived(kb.at[2, 1], num("k", 2, 1))
    peak = scores(2, 1, peak)
    last(vb, "v")
    arrived(ogb.at[0, 2], num("og", 0, 2))
    gdot(0, 2)
    arrived(ogb.at[1, 2], num("og", 1, 2))
    gdot(1, 2)
    for a in range(2):
        gs[a] = gacc[a * 256 : a * 256 + 256].astype(BF16)
        zsend(gs.at[a], gb.at[hi], "g", a)

    for s in (0, 1, 3, 2):
        arrived(vb.at[s, 1], num("v", s, 1))

    tops = [jnp.max(p, axis=0, keepdims=True) for p in peak]
    ot[...] = jnp.zeros_like(ot)

    def weigh(i, sums):
        s, r = lax.div(i, 2), lax.rem(i, 2)
        sums = list(sums)
        parts = []
        for j in range(2):
            p = jnp.exp2(st[j, i] - tops[j])
            st[j, i] = p
            sums[j] = sums[j] + jnp.sum(p.reshape(32, 8, 256), axis=0)
            parts.append(p.astype(BF16))
        ot[...] += mm(vb[s, r], jnp.concatenate(parts, axis=1), TN)
        return tuple(sums)

    sums = lax.fori_loop(0, 8, weigh, (jnp.zeros((8, 256), F32),) * 2)
    inv = [1.0 / jnp.sum(t, axis=0, keepdims=True) for t in sums]

    arrived(lr, num("lam"))
    lam_row = jnp.concatenate([lr[0:1, :], lr[0:1, :]], axis=1)
    gain_t = jnp.transpose(jnp.broadcast_to(gain[...], (128, 256)))
    gain_t = jnp.concatenate([gain_t, gain_t], axis=1)
    for a in range(2):
        arrived(gb.at[a], num("z", "g", a))

    o1 = ot[:, :256] * inv[0]
    o2 = ot[:, 256:] * inv[1]
    combined = o1 - lam_row * o2
    rms = jnp.sqrt(jnp.mean(combined * combined, axis=0, keepdims=True) + EPSILON)
    inv_rms = 1.0 / rms
    normed = combined * inv_rms
    g = jnp.concatenate([gb[0], gb[1]], axis=1).astype(F32) * (gain_t * (1.0 - LAMBDA_INIT))
    grad = ((g - normed * jnp.mean(g * normed, axis=0, keepdims=True)) * inv_rms).astype(BF16)
    gt[...] = grad
    grad32 = grad.astype(F32)
    gn[...] = jnp.transpose(grad32).astype(BF16)
    stat1 = jnp.sum(grad32 * (ot[:, :256] * inv[0]), axis=0, keepdims=True)
    stat2 = jnp.sum(grad32 * (ot[:, 256:] * inv[1]), axis=0, keepdims=True)
    inv1 = inv[0]
    inv2 = inv[1] * lam_row

    dq[...] = jnp.zeros_like(dq)

    def backward(s, r):
        i = s * 2 + r
        dp = mm(vb[s, r], gt[...])
        p1 = st[0, i] * inv1
        p2 = st[1, i] * inv2
        mixed = (p1 - p2).astype(BF16)
        ds1 = (p1 * (dp - stat1)).astype(BF16)
        ds2 = (p2 * (dp - stat2)).astype(BF16)
        dv = mm(mixed, gn[...])
        dk1 = mm(ds1, qb[:, 0:128]) * SCALE
        dk2 = mm(ds2, qb[:, 128:256]) * -SCALE
        dq[0] += mm(kb[s, r, :, 0:128], ds1, TN)
        dq[1] += mm(kb[s, r, :, 128:256], ds2, TN)
        for part, at in ((dk1, 0), (dk2, 128), (dv, 256)):
            cols = pl.ds(at, part.shape[1])
            if r:
                sibs[s, :, cols] = part.astype(BF16)
            else:
                own[s, :, cols] = part
        if r:
            send(sibs.at[s], sibr.at[s], num("sib", s), sib)

    lower, upper = pl.ds(0, 128), pl.ds(128, 128)

    def total(s, part):
        return own[s, part] + sibr[s, part].astype(F32)

    backward(2, 1)
    backward(2, 0)
    backward(1, 1)
    backward(3, 1)
    arrived(sibr.at[2], num("sib", 2))
    ys[0] = total(2, pl.ds(0, 256)).astype(BF16)
    send(ys.at[0, lower], yr.at[0], num("yr", 0), yp)
    send(ys.at[0, upper], yr.at[1], num("yr", 1), ym)
    backward(1, 0)
    arrived(sibr.at[1], num("sib", 1))
    ys[1, upper] = total(1, upper).astype(BF16)
    send(ys.at[1, upper], yf.at[0, upper], num("yf", 0, 1), yp)
    backward(3, 0)
    arrived(sibr.at[3], num("sib", 3))
    ys[2, lower] = total(3, lower).astype(BF16)
    send(ys.at[2, lower], yf.at[1, lower], num("yf", 1, 0), ym)
    backward(0, 1)
    arrived(yr.at[0], num("yr", 0))
    ys[1, lower] = (total(1, lower) + yr[0].astype(F32)).astype(BF16)
    send(ys.at[1, lower], yf.at[0, lower], num("yf", 0, 0), yp)
    arrived(yr.at[1], num("yr", 1))
    ys[2, upper] = (total(3, upper) + yr[1].astype(F32)).astype(BF16)
    send(ys.at[2, upper], yf.at[1, upper], num("yf", 1, 1), ym)
    backward(0, 0)
    for a in range(2):
        for j, sign in ((0, SCALE), (1, -SCALE)):
            dqs[a, j * 128 : j * 128 + 128] = (dq[j, :, a * 128 : a * 128 + 128] * sign).astype(BF16)
    heads_rows = pl.ds(pl.multiple_of(hi * 256, 256), 256)
    for a in range(2):
        zsend(dqs.at[a], rb.at[0, heads_rows], "dq", a)
    arrived(sibr.at[0], num("sib", 0))
    for a in range(2):
        part = pl.ds(a * 128, 128)
        for d in range(2):
            arrived(yf.at[d, part], num("yf", d, a))
        whole = total(0, part) + yf[0, part].astype(F32) + yf[1, part].astype(F32)
        dks[a] = jnp.transpose(whole).astype(BF16)
        zsend(dks.at[a, pl.ds(0, 256)], rb.at[1, heads_rows], "dk", a)
        zsend(dks.at[a, pl.ds(256, 256)], rb.at[2, heads_rows], "dv", a)

    for a in range(2):
        arrived(rb.at[0, pl.ds(a * 256, 256)], num("z", "dq", a))
    blocks = [(1, 2), (0, 2), (1, 1), (0, 3), (0, 1), (1, 3), (1, 0), (0, 0)]
    for r, s in blocks:
        w_copies[0, r, s].wait()
        pa[r, s] = mm(wb[0, r, s], rb[0])
    for a in range(2):
        arrived(rb.at[1, pl.ds(a * 256, 256)], num("z", "dk", a))
        arrived(rb.at[2, pl.ds(a * 256, 256)], num("z", "dv", a))

    def project(r, s):
        w_copies[1, r, s].wait()
        w_copies[2, r, s].wait()
        return pa[r, s] + mm(wb[1, r, s], rb[1]) + mm(wb[2, r, s], rb[2])

    xs_[1, 1] = project(1, 2).astype(BF16)
    send(xs_.at[1, 1], xr.at[1], num("xr", 1), xp)
    xs_[0, 1] = project(0, 2).astype(BF16)
    send(xs_.at[0, 1], xr.at[0], num("xr", 0), xm)
    xs_[1, 2] = project(1, 3).astype(BF16)
    send(xs_.at[1, 2], xf.at[1, 1], num("xf", 1, 1), xm)
    pa[1, 1] = project(1, 1)
    arrived(xr.at[1], num("xr", 1))
    xs_[1, 0] = (pa[1, 1] + xr[1].astype(F32)).astype(BF16)
    send(xs_.at[1, 0], xf.at[0, 1], num("xf", 0, 1), xp)
    xs_[0, 0] = project(0, 1).astype(BF16)
    send(xs_.at[0, 0], xf.at[0, 0], num("xf", 0, 0), xp)
    pa[0, 3] = project(0, 3)
    arrived(xr.at[0], num("xr", 0))
    xs_[0, 2] = (pa[0, 3] + xr[0].astype(F32)).astype(BF16)
    send(xs_.at[0, 2], xf.at[1, 0], num("xf", 1, 0), xm)
    pa[1, 0] = project(1, 0)
    pa[0, 0] = project(0, 0)
    arrived(xf.at[1, 1], num("xf", 1, 1))
    arrived(xf.at[0, 1], num("xf", 0, 1))
    zs[...] = (pa[1, 0] + xf[0, 1].astype(F32) + xf[1, 1].astype(F32)).astype(BF16)
    send(zs, zr, num("zr"), partner)
    arrived(xf.at[0, 0], num("xf", 0, 0))
    arrived(xf.at[1, 0], num("xf", 1, 0))
    arrived(zr, num("zr"))
    out[...] = (pa[0, 0] + xf[0, 0].astype(F32)) + (xf[1, 0].astype(F32) + zr[...].astype(F32))

    for cp in sent:
        cp.wait_send()


def body(order, qh, kh, vh, og, wq, wk, wv, wo, lam, gain):
    any_ = pl.BlockSpec(memory_space=pl.ANY)
    smem = pl.BlockSpec(memory_space=pltpu.SMEM)
    vmem = pl.BlockSpec(memory_space=pltpu.VMEM)
    v = pltpu.VMEM
    return pl.pallas_call(
        kernel,
        out_shape=jax.ShapeDtypeStruct((512, 128), F32),
        in_specs=[smem, smem, vmem] + [any_] * 8,
        out_specs=vmem,
        scratch_shapes=[
            v((4, 2, 256, 256), BF16),
            v((4, 2, 256, 256), BF16),
            v((256, 256), BF16),
            v((2, 256, 128), BF16),
            v((2, 256, 128), BF16),
            v((2, 4, 128, 512), BF16),
            v((2, 4, 512, 512), BF16),
            v((3, 2, 4, 512, 512), BF16),
            v((8, 128), F32),
            v((8, 128), F32),
            v((2, 8, 256, 256), F32),
            v((2, 128, 256), BF16),
            v((64, 256), jnp.int32),
            v((256, 512), F32),
            v((512, 128), F32),
            v((256, 256), BF16),
            v((256, 256), BF16),
            v((2, 128, 256), F32),
            v((4, 256, 512), BF16),
            v((4, 256, 512), BF16),
            v((4, 256, 512), F32),
            v((3, 256, 512), BF16),
            v((2, 128, 512), BF16),
            v((2, 256, 512), BF16),
            v((2, 256, 128), BF16),
            v((2, 512, 128), BF16),
            v((3, 512, 128), BF16),
            v((2, 4, 512, 128), F32),
            v((2, 3, 512, 128), BF16),
            v((2, 512, 128), BF16),
            v((2, 2, 512, 128), BF16),
            v((512, 128), BF16),
            v((512, 128), BF16),
            pltpu.SemaphoreType.DMA((4, 2, 4)),
            pltpu.SemaphoreType.DMA((1,)),
            pltpu.SemaphoreType.DMA((72,)),
            pltpu.SemaphoreType.DMA((72,)),
        ],
        compiler_params=pltpu.CompilerParams(
            collective_id=0, has_side_effects=True, vmem_limit_bytes=56 * 2**20
        ),
        name="differential_attention_backward",
    )(order, lam, gain.reshape(1, 256), qh, kh, vh, og, wq, wk, wv, wo)


def solution(mesh):
    in_specs = (
        P(),
        P("ctx", "heads"),
        P("ctx", "heads"),
        P("ctx", "heads"),
        P("ctx", "heads"),
        P(None, "heads"),
        P(None, "heads"),
        P(None, "heads"),
        P("heads", None),
        P("heads"),
        P(),
    )
    out_specs = P("heads", "ctx")
    return jax.shard_map(body, mesh=mesh, in_specs=in_specs, out_specs=out_specs, check_vma=False)
```

```python
import functools

import jax
import jax.numpy as jnp
from jax import lax
from jax.experimental import pallas as pl
from jax.experimental.pallas import tpu as pltpu
from jax.sharding import PartitionSpec as P

MESH = pl.DeviceIdType.MESH
HDIM = 128
WIDTH = 256
LAMBDA_INIT = 0.8
EPSILON = 1e-05
MASKED = -1e30
SCALE = HDIM**-0.5
LOG2E = 1.4426950408889634
F32 = jnp.float32
BF16 = jnp.bfloat16


def mm(a, b, dims=((1,), (0,))):
    return lax.dot_general(a, b, (dims, ((), ())), preferred_element_type=F32)


NT = ((1,), (1,))
TN = ((0,), (0,))


def kernel(
    order, lam, gain, qh, kh, vh, og, wq, wk, wv, wo, out, zr,
    kb, vb, qb, gs, gb, ogb, wob, wb, st, pb, qt, d0, ot, gacc, gt, gn, dq,
    sibs, sibr, own, ys, yr, dqs, dks, rb, pa, xs_, xr, xf, zs,
    wsem, lsem, ssem, rsem,
):
    ctx = lax.axis_index("ctx")
    hd = lax.axis_index("heads")
    hi = lax.div(ctx, 8)
    y = lax.rem(lax.div(ctx, 2), 4)
    c = lax.rem(ctx, 2)
    lo = lax.div(hd, 4)
    x = lax.rem(hd, 4)

    def dev(hi_, y_, c_, lo_, x_):
        return (hi_ * 8 + y_ * 2 + c_, lo_ * 4 + x_)

    sib = dev(hi, y, 1 - c, lo, x)
    ydev = {s: dev(hi, lax.rem(y + s, 4), c, lo, x) for s in (1, 2, 3)}
    xdev = {s: dev(hi, y, c, lo, lax.rem(x + s, 4)) for s in (1, 2, 3)}
    far = dev(1 - hi, y, c, lo, x)
    partner = dev(hi, y, c, 1 - lo, x)

    barrier = pltpu.get_barrier_semaphore()
    others = [sib, far, partner, *ydev.values(), *xdev.values()]
    for d in others:
        pl.semaphore_signal(barrier, inc=1, device_id=d, device_id_type=MESH)

    def half(rel):
        head = hi if rel == 0 else 1 - hi
        return pl.ds(pl.multiple_of(head * 256, 256), 256)

    count = [0]

    def load(src, dst):
        cp = pltpu.make_async_copy(src, dst, lsem.at[count[0]])
        count[0] += 1
        cp.start()
        return cp

    own_k = load(kh.at[:, half(0)], kb.at[0, 0, 0])
    own_v = load(vh.at[:, half(0)], vb.at[0, 0, 0])
    own_q = load(qh.at[:, half(0)], qb.at[pl.ds(0, 128)])
    own_og = load(og, ogb.at[0, 0])
    wo_copies = {}
    for s in range(4):
        for r in range(2):
            block = lax.rem(lo + r, 2) * 4 + lax.rem(x + s, 4)
            at = pl.ds(pl.multiple_of(block * 512, 512), 512)
            wo_copies[r, s] = load(wo.at[:, at], wob.at[r, s])
    w_copies = []
    for k, w in enumerate((wq, wk, wv)):
        for rel in range(2):
            w_copies.append(load(w.at[:, half(rel)], wb.at[k, :, pl.ds(rel * 256, 256)]))

    pl.semaphore_wait(barrier, len(others))

    used = [0]
    sent = []
    names = {}

    def num(*key):
        if key not in names:
            names[key] = len(names)
        return names[key]

    def send(src, dst, key, to):
        n = used[0]
        used[0] += 1
        cp = pltpu.make_async_remote_copy(
            src_ref=src, dst_ref=dst, send_sem=ssem.at[n], recv_sem=rsem.at[num(*key)],
            device_id=to, device_id_type=MESH,
        )
        cp.start()
        sent.append(cp)

    def arrived(dst, *key):
        pltpu.make_async_remote_copy(
            src_ref=dst, dst_ref=dst, send_sem=ssem.at[0], recv_sem=rsem.at[num(*key)],
            device_id=sib, device_id_type=MESH,
        ).wait_recv()

    def gather_y(src, buf, kind, t):
        for s in (3, 1, 2):
            send(src, buf.at[s, 0, t], (kind, s, 0, t), ydev[4 - s])

    def twin(buf, kind, s, t):
        send(buf.at[s, 0, t], buf.at[s, 1, t], (kind, s, 1, t), sib)

    def gather_x(src, r):
        for s in (3, 1, 2):
            send(src, ogb.at[r, s], ("og", r, s), xdev[4 - s])

    gather_y(kh.at[:, half(0)], kb, "k", 0)
    send(og, ogb.at[1, 0], ("og", 1, 0), partner)
    send(kh.at[:, half(1)], kb.at[0, 0, 1], ("k", 0, 0, 1), far)
    gather_x(og, 0)
    send(kh.at[:, half(0)], kb.at[0, 1, 0], ("k", 0, 1, 0), sib)
    gather_y(vh.at[:, half(0)], vb, "v", 0)
    send(vh.at[:, half(1)], vb.at[0, 0, 1], ("v", 0, 0, 1), far)
    send(qh.at[:, half(1)], qb.at[pl.ds(128, 128)], ("q",), far)
    send(vh.at[:, half(0)], vb.at[0, 1, 0], ("v", 0, 1, 0), sib)

    lane = lax.broadcasted_iota(jnp.int32, (64, 256), 1)
    row = lax.broadcasted_iota(jnp.int32, (64, 256), 0)

    def stretch(s, r, t, piece):
        token_half = hi if t == 0 else 1 - hi
        block = token_half * 8 + lax.rem(y + s, 4) * 2 + lax.rem(c + r, 2)
        return order[block * 2 + piece]

    qs = [stretch(0, 0, t, piece) for t in range(2) for piece in range(2)]
    qstretch = jnp.where(
        lane < 128,
        jnp.where(lane < 64, qs[0], qs[1]),
        jnp.where(lane < 192, qs[2], qs[3]),
    )
    d0[...] = row - qstretch * 64 - lax.rem(lane, 64)

    def scores(s, r, t, peak):
        i = (s * 2 + r) * 2 + t
        peaks = list(peak)
        for j in range(2):
            sc = mm(kb[s, r, t, :, j * 128 : j * 128 + 128], qt[j]) * (SCALE * LOG2E)
            for n in range(2):
                threshold = stretch(s, r, t, n) * -64
                part = jnp.where(d0[...] <= threshold, sc[n * 64 : n * 64 + 64], MASKED)
                st[j, i, n * 64 : n * 64 + 64] = part
                peaks[j] = jnp.maximum(peaks[j], jnp.max(part.reshape(8, 8, 256), axis=0))
        return tuple(peaks)

    def gdot(r, s, start=False):
        wo_copies[r, s].wait()
        term = mm(wob[r, s], ogb[r, s], NT)
        gacc[...] = term if start else gacc[...] + term

    arrived(kb.at[0, 0, 1], "k", 0, 0, 1)
    gather_y(kb.at[0, 0, 1], kb, "k", 1)
    twin(kb, "k", 0, 1)
    arrived(ogb.at[1, 0], "og", 1, 0)
    gather_x(ogb.at[1, 0], 1)
    arrived(vb.at[0, 0, 1], "v", 0, 0, 1)
    gather_y(vb.at[0, 0, 1], vb, "v", 1)
    twin(vb, "v", 0, 1)
    for s in (1, 3, 2):
        arrived(kb.at[s, 0, 0], "k", s, 0, 0)
        twin(kb, "k", s, 0)
    own_q.wait()
    arrived(qb.at[pl.ds(128, 128)], "q")
    for j in range(2):
        qt[j] = jnp.transpose(qb[:, j * 128 : j * 128 + 128].astype(F32)).astype(BF16)
    peak = (jnp.full((8, 256), MASKED, F32),) * 2
    own_k.wait()
    for s in (0, 1, 3, 2):
        peak = scores(s, 0, 0, peak)
    peak = scores(0, 0, 1, peak)
    for s in (1, 3, 2):
        arrived(vb.at[s, 0, 0], "v", s, 0, 0)
        twin(vb, "v", s, 0)
    own_og.wait()
    gdot(0, 0, True)
    gdot(1, 0)
    for s in (1, 3, 2):
        arrived(ogb.at[0, s], "og", 0, s)
        gdot(0, s)
    for s, t in ((0, 0), (0, 1), (1, 0), (3, 0), (2, 0)):
        arrived(kb.at[s, 1, t], "k", s, 1, t)
        peak = scores(s, 1, t, peak)
    for s in (1, 3, 2):
        arrived(kb.at[s, 0, 1], "k", s, 0, 1)
        twin(kb, "k", s, 1)
        peak = scores(s, 0, 1, peak)
    for s in (1, 3, 2):
        arrived(ogb.at[1, s], "og", 1, s)
        gdot(1, s)
    gs[...] = gacc[half(1)].astype(BF16)
    send(gs, gb.at[1], ("g",), far)
    gb[0] = gacc[half(0)].astype(BF16)
    for s in (1, 3):
        arrived(vb.at[s, 0, 1], "v", s, 0, 1)
        twin(vb, "v", s, 1)
    for s in (1, 3, 2):
        arrived(kb.at[s, 1, 1], "k", s, 1, 1)
        peak = scores(s, 1, 1, peak)

    tops = [jnp.max(p, axis=0, keepdims=True) for p in peak]

    def weigh(i, sums):
        sums = list(sums)
        for n in range(2):
            for j in range(2):
                p = jnp.exp2(st[j, 2 * i + n] - tops[j])
                st[j, 2 * i + n] = p
                sums[j] = sums[j] + jnp.sum(p.reshape(16, 8, 256), axis=0)
                pb[2 * i + n, :, j * 256 : j * 256 + 256] = p.astype(BF16)
        return tuple(sums)

    sums = lax.fori_loop(0, 8, weigh, (jnp.zeros((8, 256), F32),) * 2)
    inv = [1.0 / jnp.sum(p, axis=0, keepdims=True) for p in sums]

    def values(s, r):
        i = (s * 2 + r) * 2
        weights = pb[i : i + 2].reshape(256, 512)
        return mm(vb[s, r].reshape(256, 256), weights, TN)

    arrived(vb.at[2, 0, 1], "v", 2, 0, 1)
    twin(vb, "v", 2, 1)
    own_v.wait()
    ot[...] = values(0, 0)
    for s in (1, 3, 2):
        ot[...] += values(s, 0)
    for s in (0, 1, 3, 2):
        for t in range(2):
            arrived(vb.at[s, 1, t], "v", s, 1, t)
        ot[...] += values(s, 1)

    lam_own = lam[hi]
    gain_t = jnp.transpose(jnp.broadcast_to(gain[...], (128, 256)))
    gain_t = jnp.concatenate([gain_t, gain_t], axis=1)
    arrived(gb.at[1], "g")

    o1 = ot[:, :256] * inv[0]
    o2 = ot[:, 256:] * inv[1]
    combined = o1 - lam_own * o2
    rms = jnp.sqrt(jnp.mean(combined * combined, axis=0, keepdims=True) + EPSILON)
    inv_rms = 1.0 / rms
    normed = combined * inv_rms
    g = jnp.concatenate([gb[0], gb[1]], axis=1).astype(F32) * (gain_t * (1.0 - LAMBDA_INIT))
    grad = ((g - normed * jnp.mean(g * normed, axis=0, keepdims=True)) * inv_rms).astype(BF16)
    gt[...] = grad
    grad32 = grad.astype(F32)
    gn[...] = jnp.transpose(grad32).astype(BF16)
    stat1 = jnp.sum(grad32 * (ot[:, :256] * inv[0]), axis=0, keepdims=True)
    stat2 = jnp.sum(grad32 * (ot[:, 256:] * inv[1]), axis=0, keepdims=True)
    inv1 = inv[0]
    inv2 = inv[1] * lam_own

    dq[...] = jnp.zeros_like(dq)

    def backward(s, r, t):
        i = (s * 2 + r) * 2 + t
        dp = mm(vb[s, r, t], gt[...])
        p1 = st[0, i] * inv1
        p2 = st[1, i] * inv2
        mixed = (p1 - p2).astype(BF16)
        ds1 = (p1 * (dp - stat1)).astype(BF16)
        ds2 = (p2 * (dp - stat2)).astype(BF16)
        dv = mm(mixed, gn[...])
        dk1 = mm(ds1, qb[:, 0:128]) * SCALE
        dk2 = mm(ds2, qb[:, 128:256]) * -SCALE
        dq[0] += mm(kb[s, r, t, :, 0:128], ds1, TN)
        dq[1] += mm(kb[s, r, t, :, 128:256], ds2, TN)
        for part, at in ((dk1, 0), (dk2, 128), (dv, 256)):
            cols = pl.ds(at, part.shape[1])
            if r:
                sibs[t, s, :, cols] = part.astype(BF16)
            else:
                own[t, s, :, cols] = part
        if r:
            send(sibs.at[t, s], sibr.at[t, s], ("sib", t, s), sib)

    left, right = pl.ds(0, 256), pl.ds(256, 256)

    def total(t, s, cols):
        return own[t, s, :, cols] + sibr[t, s, :, cols].astype(F32)

    def chip_sum(t, s, cols):
        ys[t, s, :, cols] = total(t, s, cols).astype(BF16)

    def pass_on(t, s, cols, key):
        send(ys.at[t, s, :, cols], yr.at[t, s, :, cols], ("yr", t, s, key), ydev[s])

    def first_hop(t, begun=False):
        if not begun:
            backward(2, 1, t)
        backward(1, 1, t)
        backward(3, 1, t)
        backward(2, 0, t)
        arrived(sibr.at[t, 2], "sib", t, 2)
        chip_sum(t, 2, pl.ds(0, 512))
        send(ys.at[t, 2, :, left], yr.at[t, 0, :, left], ("y2", t, 0), ydev[1])
        send(ys.at[t, 2, :, right], yr.at[t, 0, :, right], ("y2", t, 1), ydev[3])
        backward(1, 0, t)
        arrived(sibr.at[t, 1], "sib", t, 1)
        chip_sum(t, 1, right)
        pass_on(t, 1, right, 1)
        backward(3, 0, t)
        arrived(sibr.at[t, 3], "sib", t, 3)
        chip_sum(t, 3, left)
        pass_on(t, 3, left, 0)
        backward(0, 1, t)
        backward(0, 0, t)

    def second_hop(t):
        arrived(yr.at[t, 0, :, left], "y2", t, 0)
        ys[t, 1, :, left] = (total(t, 1, left) + yr[t, 0, :, left].astype(F32)).astype(BF16)
        pass_on(t, 1, left, 0)
        arrived(yr.at[t, 0, :, right], "y2", t, 1)
        ys[t, 3, :, right] = (total(t, 3, right) + yr[t, 0, :, right].astype(F32)).astype(BF16)
        pass_on(t, 3, right, 1)

    def finish(t):
        arrived(sibr.at[t, 0], "sib", t, 0)
        arrived(yr.at[t, 3, :, left], "yr", t, 3, 0)
        arrived(yr.at[t, 1, :, right], "yr", t, 1, 1)
        arrived(yr.at[t, 1, :, left], "yr", t, 1, 0)
        arrived(yr.at[t, 3, :, right], "yr", t, 3, 1)
        whole = total(t, 0, pl.ds(0, 512)) + (yr[t, 1].astype(F32) + yr[t, 3].astype(F32))
        return jnp.transpose(whole).astype(BF16)

    first_hop(1)
    backward(2, 1, 0)
    second_hop(1)
    first_hop(0, True)
    for j, sign in ((0, SCALE), (1, -SCALE)):
        rb[0, 0, j * 128 : j * 128 + 128] = (dq[j, :, 0:128] * sign).astype(BF16)
        dqs[j * 128 : j * 128 + 128] = (dq[j, :, 128:256] * sign).astype(BF16)
    send(dqs, rb.at[0, 1], ("dq",), far)
    dks[...] = finish(1)
    send(dks.at[pl.ds(0, 256)], rb.at[1, 1], ("dk",), far)
    send(dks.at[pl.ds(256, 256)], rb.at[2, 1], ("dv",), far)
    second_hop(0)

    blocks = [(1, 2), (0, 2), (1, 3), (1, 1), (0, 1), (0, 3), (1, 0), (0, 0)]

    def rows(r, s):
        block = lax.rem(lo + r, 2) * 4 + lax.rem(x + s, 4)
        return pl.ds(pl.multiple_of(block * 512, 512), 512)

    for cp in w_copies:
        cp.wait()
    arrived(rb.at[0, 1], "dq")
    for r, s in blocks:
        pa[r, s] = mm(wb[0, rows(r, s)], rb[0].reshape(512, 128))
    mine = finish(0)
    rb[1, 0] = mine[:256]
    rb[2, 0] = mine[256:]
    arrived(rb.at[1, 1], "dk")
    arrived(rb.at[2, 1], "dv")

    def project(r, s):
        return (
            pa[r, s]
            + mm(wb[1, rows(r, s)], rb[1].reshape(512, 128))
            + mm(wb[2, rows(r, s)], rb[2].reshape(512, 128))
        )

    xs_[1, 1] = project(1, 2).astype(BF16)
    send(xs_.at[1, 1], xr.at[1], ("xr", 1), xdev[1])
    xs_[0, 1] = project(0, 2).astype(BF16)
    send(xs_.at[0, 1], xr.at[0], ("xr", 0), xdev[3])
    xs_[1, 2] = project(1, 3).astype(BF16)
    send(xs_.at[1, 2], xf.at[1, 1], ("xf", 1, 1), xdev[3])
    pa[1, 1] = project(1, 1)
    xs_[0, 0] = project(0, 1).astype(BF16)
    pa[0, 3] = project(0, 3)
    arrived(xr.at[1], "xr", 1)
    xs_[1, 0] = (pa[1, 1] + xr[1].astype(F32)).astype(BF16)
    send(xs_.at[1, 0], xf.at[0, 1], ("xf", 0, 1), xdev[1])
    send(xs_.at[0, 0], xf.at[0, 0], ("xf", 0, 0), xdev[1])
    arrived(xr.at[0], "xr", 0)
    xs_[0, 2] = (pa[0, 3] + xr[0].astype(F32)).astype(BF16)
    send(xs_.at[0, 2], xf.at[1, 0], ("xf", 1, 0), xdev[3])
    pa[1, 0] = project(1, 0)
    pa[0, 0] = project(0, 0)
    arrived(xf.at[1, 1], "xf", 1, 1)
    arrived(xf.at[0, 1], "xf", 0, 1)
    zs[...] = (pa[1, 0] + xf[0, 1].astype(F32) + xf[1, 1].astype(F32)).astype(BF16)
    send(zs, zr, ("zr",), partner)
    arrived(xf.at[0, 0], "xf", 0, 0)
    arrived(xf.at[1, 0], "xf", 1, 0)
    out[...] = pa[0, 0] + xf[0, 0].astype(F32) + xf[1, 0].astype(F32)
    arrived(zr, "zr")

    for cp in sent:
        cp.wait_send()


def body(order, qh, kh, vh, og, wq, wk, wv, wo, lam, gain):
    any_ = pl.BlockSpec(memory_space=pl.ANY)
    smem = pl.BlockSpec(memory_space=pltpu.SMEM)
    vmem = pl.BlockSpec(memory_space=pltpu.VMEM)
    v = pltpu.VMEM
    parts = pl.pallas_call(
        kernel,
        out_shape=(
            jax.ShapeDtypeStruct((512, 128), F32),
            jax.ShapeDtypeStruct((512, 128), BF16),
        ),
        in_specs=[smem, smem, vmem] + [any_] * 8,
        out_specs=(vmem, any_),
        scratch_shapes=[
            v((4, 2, 2, 128, 256), BF16),
            v((4, 2, 2, 128, 256), BF16),
            v((256, 256), BF16),
            v((256, 128), BF16),
            v((2, 256, 128), BF16),
            v((2, 4, 128, 512), BF16),
            v((2, 4, 512, 512), BF16),
            v((3, 4096, 512), BF16),
            v((2, 16, 128, 256), F32),
            v((16, 128, 512), BF16),
            v((2, 128, 256), BF16),
            v((64, 256), jnp.int32),
            v((256, 512), F32),
            v((512, 128), F32),
            v((256, 256), BF16),
            v((256, 256), BF16),
            v((2, 128, 256), F32),
            v((2, 4, 128, 512), BF16),
            v((2, 4, 128, 512), BF16),
            v((2, 4, 128, 512), F32),
            v((2, 4, 128, 512), BF16),
            v((2, 4, 128, 512), BF16),
            v((256, 128), BF16),
            v((512, 128), BF16),
            v((3, 2, 256, 128), BF16),
            v((2, 4, 512, 128), F32),
            v((2, 3, 512, 128), BF16),
            v((2, 512, 128), BF16),
            v((2, 2, 512, 128), BF16),
            v((512, 128), BF16),
            pltpu.SemaphoreType.DMA((1,)),
            pltpu.SemaphoreType.DMA((18,)),
            pltpu.SemaphoreType.DMA((96,)),
            pltpu.SemaphoreType.DMA((96,)),
        ],
        compiler_params=pltpu.CompilerParams(
            collective_id=0, has_side_effects=True, vmem_limit_bytes=56 * 2**20
        ),
        name="differential_attention_backward",
    )(order, lam, gain.reshape(1, 256), qh, kh, vh, og, wq, wk, wv, wo)
    return parts[0] + parts[1].astype(F32)


def solution(mesh):
    in_specs = (
        P(),
        P("ctx", "heads"),
        P("ctx", "heads"),
        P("ctx", "heads"),
        P("ctx", "heads"),
        P(None, "heads"),
        P(None, "heads"),
        P(None, "heads"),
        P("heads", None),
        P("heads"),
        P(),
    )
    out_specs = P("heads", "ctx")
    return jax.shard_map(body, mesh=mesh, in_specs=in_specs, out_specs=out_specs, check_vma=False)
```

```python
import math

import jax
import jax.numpy as jnp
from jax import lax
from jax.experimental import pallas as pl
from jax.experimental.pallas import tpu as pltpu
from jax.sharding import PartitionSpec as P

MESH = pl.DeviceIdType.MESH
HDIM = 128
WIDTH = 256
LAMBDA_INIT = 0.8
EPSILON = 1e-05
MASKED = -1e30
SCALE = HDIM**-0.5
LOG2E = 1.4426950408889634
F32 = jnp.float32
BF16 = jnp.bfloat16


def mm(a, b, dims=((1,), (0,))):
    return lax.dot_general(a, b, (dims, ((), ())), preferred_element_type=F32)


RECEIVES = 91
LOADS = 22
NT = ((1,), (1,))
TN = ((0,), (0,))


def kernel(
    order_in, lam_in, gain_in, qh, kh, vh, og, wq, wk, wv, wo, out, zr,
    order, lam, gain, kb, vb, qb, gs, gb, ogb, wob, wb, st, pb, qt, d0, ot, gacc, gt, gn, dq,
    sibs, sibr, own, ys, yr, dqs, dks, rb, pa, xs_, xr, xf, zs, ob,
    lsem, ssem, rsem,
):
    ctx = lax.axis_index("ctx")
    hd = lax.axis_index("heads")
    hi = lax.div(ctx, 8)
    y = lax.rem(lax.div(ctx, 2), 4)
    c = lax.rem(ctx, 2)
    lo = lax.div(hd, 4)
    x = lax.rem(hd, 4)

    def dev(hi_, y_, c_, lo_, x_):
        return (hi_ * 8 + y_ * 2 + c_, lo_ * 4 + x_)

    sib = dev(hi, y, 1 - c, lo, x)
    ydev = {s: dev(hi, lax.rem(y + s, 4), c, lo, x) for s in (1, 2, 3)}
    xdev = {s: dev(hi, y, c, lo, lax.rem(x + s, 4)) for s in (1, 2, 3)}
    far = dev(1 - hi, y, c, lo, x)
    partner = dev(hi, y, c, 1 - lo, x)

    barrier = pltpu.get_barrier_semaphore()
    others = [sib, far, partner, *ydev.values(), *xdev.values()]
    for d in others:
        pl.semaphore_signal(barrier, inc=1, device_id=d, device_id_type=MESH)

    def half(rel):
        head = hi if rel == 0 else 1 - hi
        return pl.ds(pl.multiple_of(head * 256, 256), 256)

    count = [0]

    def load(src, dst):
        cp = pltpu.make_async_copy(src, dst, lsem.at[count[0]])
        count[0] += 1
        cp.start()
        return cp

    small = [load(order_in, order), load(lam_in, lam), load(gain_in, gain)]
    own_k = load(kh.at[:, half(0)], kb.at[0, 0, 0])
    own_v = load(vh.at[:, half(0)], vb.at[0, 0, 0])
    own_q = load(qh.at[:, half(0)], qb.at[pl.ds(0, 128)])
    own_og = load(og, ogb.at[0, 0])
    wo_copies = {}
    for s in range(4):
        for r in range(2):
            block = lax.rem(lo + r, 2) * 4 + lax.rem(x + s, 4)
            at = pl.ds(pl.multiple_of(block * 512, 512), 512)
            wo_copies[r, s] = load(wo.at[:, at], wob.at[r, s])
    w_copies = []
    for w, rel, group, at in (
        (wq, 0, 0, 0), (wq, 1, 0, 256), (wk, 0, 1, 0), (wv, 0, 1, 256), (wk, 1, 2, 0), (wv, 1, 2, 256),
    ):
        w_copies.append(load(w.at[:, half(rel)], wb.at[group, :, pl.ds(at, 256)]))

    pl.semaphore_wait(barrier, len(others))

    names = {}
    sent = [0]

    def num(*key):
        if key not in names:
            names[key] = len(names)
        return names[key]

    def send(src, dst, key, to):
        pltpu.make_async_remote_copy(
            src_ref=src, dst_ref=dst, send_sem=ssem.at[0], recv_sem=rsem.at[num(*key)],
            device_id=to, device_id_type=MESH,
        ).start()
        sent[0] += math.prod(src.shape) * src.dtype.itemsize

    def all_sent():
        rows = wb.at[0, pl.ds(0, sent[0] // 1024)]
        pltpu.make_async_remote_copy(
            src_ref=rows, dst_ref=rows, send_sem=ssem.at[0], recv_sem=rsem.at[0],
            device_id=sib, device_id_type=MESH,
        ).wait_send()
        sent[0] = 0

    def arrived(dst, *key):
        pltpu.make_async_remote_copy(
            src_ref=dst, dst_ref=dst, send_sem=ssem.at[0], recv_sem=rsem.at[num(*key)],
            device_id=sib, device_id_type=MESH,
        ).wait_recv()

    def gather_y(src, buf, kind, t, steps=(2, 3, 1)):
        for s in steps:
            send(src, buf.at[t, s, 0], (kind, s, 0, t), ydev[4 - s])

    def twin(buf, kind, s, t):
        send(buf.at[t, s, 0], buf.at[t, s, 1], (kind, s, 1, t), sib)

    def gather_x(src, r, steps=(2, 3, 1)):
        for s in steps:
            send(src, ogb.at[r, s], ("og", r, s), xdev[4 - s])

    send(kh.at[:, half(1)], kb.at[1, 0, 0], ("k", 0, 0, 1), far)
    send(og, ogb.at[1, 0], ("og", 1, 0), partner)
    gather_y(kh.at[:, half(0)], kb, "k", 0)
    gather_x(og, 0)
    send(vh.at[:, half(1)], vb.at[1, 0, 0], ("v", 0, 0, 1), far)
    gather_y(vh.at[:, half(0)], vb, "v", 0, (3, 1))
    send(qh.at[:, half(1)], qb.at[pl.ds(128, 128)], ("q",), far)
    send(kh.at[:, half(0)], kb.at[0, 0, 1], ("k", 0, 1, 0), sib)
    send(vh.at[:, half(0)], vb.at[0, 0, 1], ("v", 0, 1, 0), sib)

    for cp in small:
        cp.wait()
    lane = lax.broadcasted_iota(jnp.int32, (64, 256), 1)
    row = lax.broadcasted_iota(jnp.int32, (64, 256), 0)

    def stretch(s, r, t, piece):
        token_half = hi if t == 0 else 1 - hi
        block = token_half * 8 + lax.rem(y + s, 4) * 2 + lax.rem(c + r, 2)
        return order[block * 2 + piece]

    qs = [stretch(0, 0, t, piece) for t in range(2) for piece in range(2)]
    qstretch = jnp.where(
        lane < 128,
        jnp.where(lane < 64, qs[0], qs[1]),
        jnp.where(lane < 192, qs[2], qs[3]),
    )
    d0[...] = row - qstretch * 64 - lax.rem(lane, 64)

    def scores(s, r, t, peak):
        i = s * 2 + r
        peaks = list(peak)
        for j in range(2):
            sc = mm(kb[t, s, r, :, j * 128 : j * 128 + 128], qt[j]) * (SCALE * LOG2E)
            for n in range(2):
                threshold = stretch(s, r, t, n) * -64
                part = jnp.where(d0[...] <= threshold, sc[n * 64 : n * 64 + 64], MASKED)
                st[j, t, i, n * 64 : n * 64 + 64] = part
                peaks[j] = jnp.maximum(peaks[j], jnp.max(part.reshape(8, 8, 256), axis=0))
        return tuple(peaks)

    def gdot(r, s, start=False):
        wo_copies[r, s].wait()
        term = mm(wob[r, s], ogb[r, s], NT)
        gacc[...] = term if start else gacc[...] + term

    arrived(kb.at[1, 0, 0], "k", 0, 0, 1)
    gather_y(kb.at[1, 0, 0], kb, "k", 1)
    twin(kb, "k", 0, 1)
    arrived(ogb.at[1, 0], "og", 1, 0)
    gather_x(ogb.at[1, 0], 1, (3, 1))
    arrived(ogb.at[0, 2], "og", 0, 2)
    send(ogb.at[0, 2], ogb.at[1, 2], ("og", 1, 2), partner)
    for s in (1, 3, 2):
        arrived(kb.at[0, s, 0], "k", s, 0, 0)
        twin(kb, "k", s, 0)
    lower, upper = pl.ds(0, 64), pl.ds(64, 64)
    for s, part, to in ((3, lower, 1), (1, upper, 3)):
        arrived(vb.at[0, s, 0], "v", s, 0, 0)
        send(vb.at[0, s, 0, part], vb.at[0, 2, 0, part], ("v", 2, 0, 0, s), ydev[to])
        twin(vb, "v", s, 0)
    own_og.wait()
    gdot(0, 0, True)
    gdot(1, 0)
    gdot(0, 2)
    arrived(vb.at[1, 0, 0], "v", 0, 0, 1)
    gather_y(vb.at[1, 0, 0], vb, "v", 1)
    twin(vb, "v", 0, 1)
    for s in (1, 3):
        arrived(ogb.at[0, s], "og", 0, s)
        gdot(0, s)
    own_q.wait()
    arrived(qb.at[pl.ds(128, 128)], "q")
    for j in range(2):
        qt[j] = jnp.transpose(qb[:, j * 128 : j * 128 + 128].astype(F32)).astype(BF16)
    peak = (jnp.full((8, 256), MASKED, F32),) * 2
    own_k.wait()
    for s in (0, 1, 3, 2):
        peak = scores(s, 0, 0, peak)
    for s in (1, 3, 2):
        arrived(kb.at[1, s, 0], "k", s, 0, 1)
        twin(kb, "k", s, 1)
    for s in (1, 3, 2):
        arrived(ogb.at[1, s], "og", 1, s)
        gdot(1, s)
    gs[...] = gacc[half(1)].astype(BF16)
    send(gs, gb.at[1], ("g",), far)
    gb[0] = gacc[half(0)].astype(BF16)
    for s, part in ((3, lower), (1, upper)):
        arrived(vb.at[0, 2, 0, part], "v", 2, 0, 0, s)
    twin(vb, "v", 2, 0)
    for s in (0, 1, 3, 2):
        peak = scores(s, 0, 1, peak)
    for s in (0, 1, 3, 2):
        arrived(kb.at[0, s, 1], "k", s, 1, 0)
        peak = scores(s, 1, 0, peak)
    for s in (1, 3):
        arrived(vb.at[1, s, 0], "v", s, 0, 1)
        twin(vb, "v", s, 1)
    for s in (0, 1, 3, 2):
        arrived(kb.at[1, s, 1], "k", s, 1, 1)
        peak = scores(s, 1, 1, peak)

    tops = [jnp.max(p, axis=0, keepdims=True) for p in peak]

    def weigh(i, sums):
        sums = list(sums)
        for t in range(2):
            for j in range(2):
                p = jnp.exp2(st[j, t, i] - tops[j])
                st[j, t, i] = p
                sums[j] = sums[j] + jnp.sum(p.reshape(16, 8, 256), axis=0)
                pb[t, i, :, j * 256 : j * 256 + 256] = p.astype(BF16)
        return tuple(sums)

    sums = lax.fori_loop(0, 8, weigh, (jnp.zeros((8, 256), F32),) * 2)
    inv = [1.0 / jnp.sum(p, axis=0, keepdims=True) for p in sums]

    def values(t, s):
        return mm(vb[t, s].reshape(256, 256), pb[t, 2 * s : 2 * s + 2].reshape(256, 512), TN)

    arrived(vb.at[1, 2, 0], "v", 2, 0, 1)
    twin(vb, "v", 2, 1)
    own_v.wait()
    for s in (0, 1, 3, 2):
        arrived(vb.at[0, s, 1], "v", s, 1, 0)
    ot[...] = mm(vb[0].reshape(1024, 256), pb[0].reshape(1024, 512), TN)
    for s in (0, 1, 3, 2):
        arrived(vb.at[1, s, 1], "v", s, 1, 1)
        ot[...] += values(1, s)

    lam_own = lam[hi]
    gain_t = jnp.transpose(jnp.broadcast_to(gain[...], (128, 256)))
    gain_t = jnp.concatenate([gain_t, gain_t], axis=1)
    arrived(gb.at[1], "g")

    o1 = ot[:, :256] * inv[0]
    o2 = ot[:, 256:] * inv[1]
    combined = o1 - lam_own * o2
    rms = jnp.sqrt(jnp.mean(combined * combined, axis=0, keepdims=True) + EPSILON)
    inv_rms = 1.0 / rms
    normed = combined * inv_rms
    g = jnp.concatenate([gb[0], gb[1]], axis=1).astype(F32) * (gain_t * (1.0 - LAMBDA_INIT))
    grad = ((g - normed * jnp.mean(g * normed, axis=0, keepdims=True)) * inv_rms).astype(BF16)
    gt[...] = grad
    grad32 = grad.astype(F32)
    gn[...] = jnp.transpose(grad32).astype(BF16)
    stat1 = jnp.sum(grad32 * (ot[:, :256] * inv[0]), axis=0, keepdims=True)
    stat2 = jnp.sum(grad32 * (ot[:, 256:] * inv[1]), axis=0, keepdims=True)
    inv1 = inv[0]
    inv2 = inv[1] * lam_own

    dq[...] = jnp.zeros_like(dq)

    def backward(s, r):
        i = s * 2 + r
        dp = mm(vb[:, s, r].reshape(256, 256), gt[...])
        keys = kb[:, s, r].reshape(256, 256)
        p1 = st[0, :, i].reshape(256, 256) * inv1
        p2 = st[1, :, i].reshape(256, 256) * inv2
        mixed = (p1 - p2).astype(BF16)
        ds1 = (p1 * (dp - stat1)).astype(BF16)
        ds2 = (p2 * (dp - stat2)).astype(BF16)
        dv = mm(mixed, gn[...])
        dk1 = mm(ds1, qb[:, 0:128]) * SCALE
        dk2 = mm(ds2, qb[:, 128:256]) * -SCALE
        dq[0] += mm(keys[:, 0:128], ds1, TN)
        dq[1] += mm(keys[:, 128:256], ds2, TN)
        for part, at in ((dk1, 0), (dk2, 128), (dv, 256)):
            cols = pl.ds(at, part.shape[1])
            for t in range(2):
                piece = part[t * 128 : t * 128 + 128]
                if r:
                    sibs[s, t, :, cols] = piece.astype(BF16)
                else:
                    own[t, s, :, cols] = piece
        if r:
            send(sibs.at[s], sibr.at[s], ("sib", s), sib)

    both = pl.ds(0, 512)
    ups = {0: [pl.ds(0, 256)], 1: [pl.ds(0, 128), pl.ds(128, 128)]}
    downs = {0: [pl.ds(256, 256)], 1: [pl.ds(256, 128), pl.ds(384, 128)]}

    def total(t, s, cols):
        return own[t, s, :, cols] + sibr[s, t, :, cols].astype(F32)

    def chip_sum(t, s, cols):
        ys[t, s, :, cols] = total(t, s, cols).astype(BF16)

    def pass_on(t, s, cols, *key):
        send(ys.at[t, s, :, cols], yr.at[t, s, :, cols], ("yr", t, s, *key), ydev[s])

    def first_hop(t):
        chip_sum(t, 2, both)
        for n, (up, down) in enumerate(zip(ups[t], downs[t])):
            send(ys.at[t, 2, :, up], yr.at[t, 0, :, up], ("y2", t, 0, n), ydev[1])
            send(ys.at[t, 2, :, down], yr.at[t, 0, :, down], ("y2", t, 1, n), ydev[3])

    def straight(t, s):
        cols = pl.ds(256, 256) if s == 1 else pl.ds(0, 256)
        chip_sum(t, s, cols)
        pass_on(t, s, cols, "direct")

    def second_hop(t):
        for n, (up, down) in enumerate(zip(ups[t], downs[t])):
            for s, cols, way in ((1, up, 0), (3, down, 1)):
                arrived(yr.at[t, 0, :, cols], "y2", t, way, n)
                ys[t, s, :, cols] = (total(t, s, cols) + yr[t, 0, :, cols].astype(F32)).astype(BF16)
                pass_on(t, s, cols, n)

    def finish(t, n, cols, s):
        arrived(yr.at[t, s, :, cols], "yr", t, s, n)
        whole = total(t, 0, cols) + (yr[t, 1, :, cols].astype(F32) + yr[t, 3, :, cols].astype(F32))
        return jnp.transpose(whole).astype(BF16)

    def finish_direct(t):
        arrived(yr.at[t, 3, :, pl.ds(0, 256)], "yr", t, 3, "direct")
        arrived(yr.at[t, 1, :, pl.ds(256, 256)], "yr", t, 1, "direct")

    all_sent()
    backward(2, 1)
    backward(2, 0)
    backward(1, 1)
    backward(3, 1)
    arrived(sibr.at[2], "sib", 2)
    first_hop(1)
    backward(1, 0)
    arrived(sibr.at[1], "sib", 1)
    straight(1, 1)
    backward(3, 0)
    arrived(sibr.at[3], "sib", 3)
    straight(1, 3)
    first_hop(0)
    backward(0, 1)
    backward(0, 0)
    for j, sign in ((0, SCALE), (1, -SCALE)):
        rb[0, j * 128 : j * 128 + 128] = (dq[j, :, 0:128] * sign).astype(BF16)
        dqs[j * 128 : j * 128 + 128] = (dq[j, :, 128:256] * sign).astype(BF16)
    send(dqs, rb.at[0, pl.ds(256, 256)], ("dq",), far)
    straight(0, 1)
    straight(0, 3)
    second_hop(1)
    arrived(sibr.at[0], "sib", 0)
    finish_direct(1)
    second_hop(0)
    for n, (up, down) in enumerate(zip(ups[1], downs[1])):
        for s, cols in ((1, up), (3, down)):
            dks[cols, :] = finish(1, n, cols, s)
            send(dks.at[cols], rb.at[2, cols], ("dk", n, s), far)

    blocks = [(1, 2), (1, 1), (1, 3), (0, 2), (0, 1), (0, 3), (1, 0), (0, 0)]

    def rows(r, s):
        block = lax.rem(lo + r, 2) * 4 + lax.rem(x + s, 4)
        return pl.ds(pl.multiple_of(block * 512, 512), 512)

    for cp in w_copies:
        cp.wait()
    arrived(rb.at[0, pl.ds(256, 256)], "dq")
    for r, s in blocks:
        pa[r, s] = mm(wb[0, rows(r, s)], rb[0])
    finish_direct(0)
    for s, cols in ((1, ups[0][0]), (3, downs[0][0])):
        rb[1, cols, :] = finish(0, 0, cols, s)
    early = blocks[:2]
    for r, s in early:
        pa[r, s] += mm(wb[1, rows(r, s)], rb[1])
    for n in range(2):
        for s, cols in ((1, ups[1][n]), (3, downs[1][n])):
            arrived(rb.at[2, cols], "dk", n, s)

    def project(r, s):
        near = 0 if (r, s) in early else mm(wb[1, rows(r, s)], rb[1])
        return pa[r, s] + (near + mm(wb[2, rows(r, s)], rb[2]))

    def tops_of(q):
        return pl.ds(q * 256, 128)

    def bottoms_of(q):
        return pl.ds(q * 256 + 128, 128)

    def x_first(r):
        xs_[r, 2] = project(r, 2).astype(BF16)
        for q in range(2):
            for part, way, to in ((tops_of(q), 0, 1), (bottoms_of(q), 1, 3)):
                send(xs_.at[r, 2, part], xr.at[r, part], ("xr", r, q, way), xdev[to])

    def x_pass(r, s, part, *key):
        send(xs_.at[r, s, part], xf.at[s // 2, r, part], ("xf", s, r, *key), xdev[s])

    def x_direct(r):
        for q in range(2):
            for s, part in ((1, bottoms_of(q)), (3, tops_of(q))):
                xs_[r, s, part] = pa[r, s, part].astype(BF16)
                x_pass(r, s, part, q, 0)

    def x_second(r, q):
        for s, part, way in ((1, tops_of(q), 0), (3, bottoms_of(q), 1)):
            arrived(xr.at[r, part], "xr", r, q, way)
            xs_[r, s, part] = (pa[r, s, part] + xr[r, part].astype(F32)).astype(BF16)
            x_pass(r, s, part, q, 1)

    def x_final(r, q):
        for s, part, n in (
            (1, bottoms_of(q), 0), (3, tops_of(q), 0), (1, tops_of(q), 1), (3, bottoms_of(q), 1),
        ):
            arrived(xf.at[s // 2, r, part], "xf", s, r, q, n)
        part = pl.ds(q * 256, 256)
        return pa[r, 0, part] + (xf[0, r, part].astype(F32) + xf[1, r, part].astype(F32))

    x_first(1)
    pa[1, 1] = project(1, 1)
    pa[1, 3] = project(1, 3)
    x_direct(1)
    x_first(0)
    for r, s in ((0, 1), (0, 3), (1, 0), (0, 0)):
        pa[r, s] = project(r, s)
    x_second(1, 0)
    x_second(1, 1)
    x_direct(0)
    x_second(0, 0)
    x_second(0, 1)
    for q in range(2):
        part = pl.ds(q * 256, 256)
        zs[part, :] = x_final(1, q).astype(BF16)
        send(zs.at[part], zr.at[part], ("zr", q), partner)
    for q in range(2):
        ob[pl.ds(q * 256, 256), :] = x_final(0, q)
    done = load(ob, out)
    all_sent()
    done.wait()
    for q in range(2):
        arrived(zr.at[pl.ds(q * 256, 256)], "zr", q)
    assert (len(names), count[0]) == (RECEIVES, LOADS), (len(names), count[0])


def body(order, qh, kh, vh, og, wq, wk, wv, wo, lam, gain):
    any_ = pl.BlockSpec(memory_space=pl.ANY)
    v = pltpu.VMEM
    parts = pl.pallas_call(
        kernel,
        out_shape=(
            jax.ShapeDtypeStruct((512, 128), F32),
            jax.ShapeDtypeStruct((512, 128), BF16),
        ),
        in_specs=[any_] * 11,
        out_specs=(any_, any_),
        scratch_shapes=[
            pltpu.SMEM((32,), jnp.int32),
            pltpu.SMEM((2,), F32),
            v((1, 256), F32),
            v((2, 4, 2, 128, 256), BF16),
            v((2, 4, 2, 128, 256), BF16),
            v((256, 256), BF16),
            v((256, 128), BF16),
            v((2, 256, 128), BF16),
            v((2, 4, 128, 512), BF16),
            v((2, 4, 512, 512), BF16),
            v((3, 4096, 512), BF16),
            v((2, 2, 8, 128, 256), F32),
            v((2, 8, 128, 512), BF16),
            v((2, 128, 256), BF16),
            v((64, 256), jnp.int32),
            v((256, 512), F32),
            v((512, 128), F32),
            v((256, 256), BF16),
            v((256, 256), BF16),
            v((2, 128, 256), F32),
            v((4, 2, 128, 512), BF16),
            v((4, 2, 128, 512), BF16),
            v((2, 4, 128, 512), F32),
            v((2, 4, 128, 512), BF16),
            v((2, 4, 128, 512), BF16),
            v((256, 128), BF16),
            v((512, 128), BF16),
            v((3, 512, 128), BF16),
            v((2, 4, 512, 128), F32),
            v((2, 4, 512, 128), BF16),
            v((2, 512, 128), BF16),
            v((2, 2, 512, 128), BF16),
            v((512, 128), BF16),
            v((512, 128), F32),
            pltpu.SemaphoreType.DMA((LOADS,)),
            pltpu.SemaphoreType.DMA((1,)),
            pltpu.SemaphoreType.DMA((RECEIVES,)),
        ],
        compiler_params=pltpu.CompilerParams(
            collective_id=0, has_side_effects=True, vmem_limit_bytes=56 * 2**20
        ),
        name="differential_attention_backward",
    )(order, lam, gain.reshape(1, 256), qh, kh, vh, og, wq, wk, wv, wo)
    return parts[0] + parts[1].astype(F32)


def solution(mesh):
    in_specs = (
        P(),
        P("ctx", "heads"),
        P("ctx", "heads"),
        P("ctx", "heads"),
        P("ctx", "heads"),
        P(None, "heads"),
        P(None, "heads"),
        P(None, "heads"),
        P("heads", None),
        P("heads"),
        P(),
    )
    out_specs = P("heads", "ctx")
    return jax.shard_map(body, mesh=mesh, in_specs=in_specs, out_specs=out_specs, check_vma=False)
```

```python
import math

import jax
import jax.numpy as jnp
from jax import lax
from jax.experimental import pallas as pl
from jax.experimental.pallas import tpu as pltpu
from jax.sharding import PartitionSpec as P

MESH = pl.DeviceIdType.MESH
HDIM = 128
WIDTH = 256
LAMBDA_INIT = 0.8
EPSILON = 1e-05
MASKED = -1e30
SCALE = HDIM**-0.5
LOG2E = 1.4426950408889634
F32 = jnp.float32
BF16 = jnp.bfloat16


def mm(a, b, dims=((1,), (0,))):
    return lax.dot_general(a, b, (dims, ((), ())), preferred_element_type=F32)


RECEIVES = 42
LOADS = 7
NT = ((1,), (1,))
TN = ((0,), (0,))


def kernel(
    order_in, lam_in, gain_in, qh, kh, vh, og, wq, wk, wv, wo, out, zr,
    order, lam, gain, kb, vb, qb, gs, gb, ogb, wob, wb, st, pb, qt, d0, ot, gacc, gt, gn, dq,
    sibs, sibr, own, ys, yr, dqs, dks, rb, pa, xs_, xr, xf, zs, ob,
    lsem, ssem, rsem,
):
    ctx = lax.axis_index("ctx")
    hd = lax.axis_index("heads")
    hi = lax.div(ctx, 8)
    y = lax.rem(lax.div(ctx, 2), 4)
    c = lax.rem(ctx, 2)
    lo = lax.div(hd, 4)
    x = lax.rem(hd, 4)

    def dev(hi_, y_, c_, lo_, x_):
        return (hi_ * 8 + y_ * 2 + c_, lo_ * 4 + x_)

    sib = dev(hi, y, 1 - c, lo, x)
    ydev = {s: dev(hi, lax.rem(y + s, 4), c, lo, x) for s in (1, 2, 3)}
    xdev = {s: dev(hi, y, c, lo, lax.rem(x + s, 4)) for s in (1, 2, 3)}
    far = dev(1 - hi, y, c, lo, x)
    partner = dev(hi, y, c, 1 - lo, x)

    barrier = pltpu.get_barrier_semaphore()
    others = [sib, far, partner, *ydev.values(), *xdev.values()]
    for d in others:
        pl.semaphore_signal(barrier, inc=1, device_id=d, device_id_type=MESH)

    def half(rel):
        head = hi if rel == 0 else 1 - hi
        return pl.ds(pl.multiple_of(head * 256, 256), 256)

    def load(src, dst, n):
        cp = pltpu.make_async_copy(src, dst, lsem.at[n])
        cp.start()
        return cp

    small = [load(order_in, order, 0), load(lam_in, lam, 1), load(gain_in, gain, 2)]
    load(kh.at[:, half(0)], kb.at[0, 0, 0], 3)
    load(vh.at[:, half(0)], vb.at[0, 0, 0], 3)
    load(qh.at[:, half(0)], qb.at[pl.ds(0, 128)], 3)
    load(og, ogb.at[0, 0], 3)
    for s in range(4):
        for r in range(2):
            block = lax.rem(lo + r, 2) * 4 + lax.rem(x + s, 4)
            at = pl.ds(pl.multiple_of(block * 512, 512), 512)
            load(wo.at[:, at], wob.at[r, s], 4)
    for w, rel, group, at in (
        (wq, 0, 0, 0), (wq, 1, 0, 256), (wk, 0, 1, 0), (wv, 0, 1, 256), (wk, 1, 2, 0), (wv, 1, 2, 256),
    ):
        load(w.at[:, half(rel)], wb.at[group, :, pl.ds(at, 256)], 5)

    def loaded(ref, n):
        pltpu.make_async_copy(ref, ref, lsem.at[n]).wait()

    pl.semaphore_wait(barrier, len(others))

    names = {}
    sent = [0]

    def num(*key):
        if key not in names:
            names[key] = len(names)
        return names[key]

    def send(src, dst, key, to):
        pltpu.make_async_remote_copy(
            src_ref=src, dst_ref=dst, send_sem=ssem.at[0], recv_sem=rsem.at[num(*key)],
            device_id=to, device_id_type=MESH,
        ).start()
        sent[0] += math.prod(src.shape) * src.dtype.itemsize

    def all_sent():
        rows = wb.at[0, pl.ds(0, sent[0] // 1024)]
        pltpu.make_async_remote_copy(
            src_ref=rows, dst_ref=rows, send_sem=ssem.at[0], recv_sem=rsem.at[0],
            device_id=sib, device_id_type=MESH,
        ).wait_send()
        sent[0] = 0

    def arrived(dst, *key):
        pltpu.make_async_remote_copy(
            src_ref=dst, dst_ref=dst, send_sem=ssem.at[0], recv_sem=rsem.at[num(*key)],
            device_id=sib, device_id_type=MESH,
        ).wait_recv()

    def gather_y(src, buf, key, t, steps=(2, 3, 1)):
        for s in steps:
            send(src, buf.at[t, s, 0], (*key, s) if len(key) > 1 else key, ydev[4 - s])

    def twin(buf, s, t, *key):
        send(buf.at[t, s, 0], buf.at[t, s, 1], key, sib)

    def gather_x(src, r, steps=(2, 3, 1)):
        for s in steps:
            send(src, ogb.at[r, s], ("og", r, s == 2), xdev[4 - s])

    send(kh.at[:, half(1)], kb.at[1, 0, 0], ("k far",), far)
    send(og, ogb.at[1, 0], ("og partner",), partner)
    gather_y(kh.at[:, half(0)], kb, ("k0",), 0)
    gather_x(og, 0)
    send(vh.at[:, half(1)], vb.at[1, 0, 0], ("v far",), far)
    gather_y(vh.at[:, half(0)], vb, ("v0",), 0, (3, 1))
    send(qh.at[:, half(1)], qb.at[pl.ds(128, 128)], ("q",), far)
    send(kh.at[:, half(0)], kb.at[0, 0, 1], ("k0 twin",), sib)
    send(vh.at[:, half(0)], vb.at[0, 0, 1], ("v0 twin",), sib)

    for cp in small:
        cp.wait()
    lane = lax.broadcasted_iota(jnp.int32, (64, 256), 1)
    row = lax.broadcasted_iota(jnp.int32, (64, 256), 0)

    def stretch(s, r, t, piece):
        token_half = hi if t == 0 else 1 - hi
        block = token_half * 8 + lax.rem(y + s, 4) * 2 + lax.rem(c + r, 2)
        return order[block * 2 + piece]

    qs = [stretch(0, 0, t, piece) for t in range(2) for piece in range(2)]
    qstretch = jnp.where(
        lane < 128,
        jnp.where(lane < 64, qs[0], qs[1]),
        jnp.where(lane < 192, qs[2], qs[3]),
    )
    d0[...] = row - qstretch * 64 - lax.rem(lane, 64)

    def scores(s, t, peak):
        peaks = list(peak)
        for j in range(2):
            keys = kb[t, s].reshape(256, 256)[:, j * 128 : j * 128 + 128]
            sc = mm(keys, qt[j]) * (SCALE * LOG2E)
            for n in range(4):
                threshold = stretch(s, n // 2, t, n % 2) * -64
                part = jnp.where(d0[...] <= threshold, sc[n * 64 : n * 64 + 64], MASKED)
                at = pl.ds(n % 2 * 64, 64)
                st[j, t, s * 2 + n // 2, at] = part
                peaks[j] = jnp.maximum(peaks[j], jnp.max(part.reshape(8, 8, 256), axis=0))
        return tuple(peaks)

    def gdot(r, s, head=None, start=False):
        rows = pl.ds(0, 512) if head is None else half(head)
        term = mm(wob[r, s, rows], ogb[r, s], NT)
        gacc[rows] = term if start else gacc[rows] + term

    arrived(kb.at[1, 0, 0], "k far")
    gather_y(kb.at[1, 0, 0], kb, ("k1",), 1)
    twin(kb, 0, 1, "k1 twin")
    arrived(ogb.at[1, 0], "og partner")
    gather_x(ogb.at[1, 0], 1, (3, 1))
    arrived(ogb.at[0, 2], "og", 0, True)
    send(ogb.at[0, 2], ogb.at[1, 2], ("og", 1, True), partner)
    arrived(kb.at[0, pl.ds(1, 3), 0], "k0")
    for s in (1, 3, 2):
        twin(kb, s, 0, "k0 twin")
    lower, upper = pl.ds(0, 64), pl.ds(64, 64)
    arrived(vb.at[0, pl.ds(1, 2), 0], "v0")
    for s, part, to in ((3, lower, 1), (1, upper, 3)):
        send(vb.at[0, s, 0, part], vb.at[0, 2, 0, part], ("v0 relay",), ydev[to])
        twin(vb, s, 0, "v0 twin")
    loaded(wb.at[0, pl.ds(0, 320)], 3)
    loaded(wob, 4)
    gdot(0, 0, start=True)
    gdot(1, 0)
    gdot(0, 2)
    arrived(vb.at[1, 0, 0], "v far")
    gather_y(vb.at[1, 0, 0], vb, ("v1", "y"), 1)
    twin(vb, 0, 1, "v1 twin", 0)
    arrived(ogb.at[0, pl.ds(0, 2)], "og", 0, False)
    gdot(0, 1)
    gdot(0, 3)
    arrived(qb.at[pl.ds(128, 128)], "q")
    for j in range(2):
        qt[j] = jnp.transpose(qb[:, j * 128 : j * 128 + 128].astype(F32)).astype(BF16)
    peak = (jnp.full((8, 256), MASKED, F32),) * 2
    arrived(kb.at[0, :, 1], "k0 twin")
    for s in (0, 1):
        peak = scores(s, 0, peak)
    arrived(kb.at[1, pl.ds(1, 3), 0], "k1")
    for s in (1, 3, 2):
        twin(kb, s, 1, "k1 twin")
    arrived(ogb.at[1, pl.ds(0, 2)], "og", 1, False)
    arrived(ogb.at[1, 2], "og", 1, True)
    for s in (1, 3, 2):
        gdot(1, s, 1)
    gs[...] = gacc[half(1)].astype(BF16)
    send(gs, gb.at[1], ("g",), far)
    for s in (1, 3, 2):
        gdot(1, s, 0)
    gb[0] = gacc[half(0)].astype(BF16)
    arrived(vb.at[0, 2, 0], "v0 relay")
    twin(vb, 2, 0, "v0 twin")
    for s in (3, 2):
        peak = scores(s, 0, peak)
    for s in (1, 3):
        arrived(vb.at[1, s, 0], "v1", "y", s)
        twin(vb, s, 1, "v1 twin", 0)
    arrived(kb.at[1, :, 1], "k1 twin")
    for s in range(4):
        peak = scores(s, 1, peak)

    tops = [jnp.max(p, axis=0, keepdims=True) for p in peak]

    def weigh(i, sums):
        sums = list(sums)
        for t in range(2):
            for j in range(2):
                p = jnp.exp2(st[j, t, i] - tops[j])
                st[j, t, i] = p
                sums[j] = sums[j] + jnp.sum(p.reshape(16, 8, 256), axis=0)
                pb[t, i, :, j * 256 : j * 256 + 256] = p.astype(BF16)
        return tuple(sums)

    sums = lax.fori_loop(0, 8, weigh, (jnp.zeros((8, 256), F32),) * 2)
    inv = [1.0 / jnp.sum(p, axis=0, keepdims=True) for p in sums]

    def values(t, s):
        return mm(vb[t, s].reshape(256, 256), pb[t, 2 * s : 2 * s + 2].reshape(256, 512), TN)

    arrived(vb.at[1, 2, 0], "v1", "y", 2)
    twin(vb, 2, 1, "v1 twin", 1)
    arrived(vb.at[0, :, 1], "v0 twin")
    ot[...] = mm(vb[0].reshape(1024, 256), pb[0].reshape(1024, 512), TN)
    arrived(vb.at[1, pl.ds(0, 3), 1], "v1 twin", 0)
    for s in (0, 1, 3):
        ot[...] += values(1, s)
    arrived(vb.at[1, 2, 1], "v1 twin", 1)
    ot[...] += values(1, 2)

    lam_own = lam[hi]
    gain_t = jnp.transpose(jnp.broadcast_to(gain[...], (128, 256)))
    gain_t = jnp.concatenate([gain_t, gain_t], axis=1)
    arrived(gb.at[1], "g")

    o1 = ot[:, :256] * inv[0]
    o2 = ot[:, 256:] * inv[1]
    combined = o1 - lam_own * o2
    rms = jnp.sqrt(jnp.mean(combined * combined, axis=0, keepdims=True) + EPSILON)
    inv_rms = 1.0 / rms
    normed = combined * inv_rms
    g = jnp.concatenate([gb[0], gb[1]], axis=1).astype(F32) * (gain_t * (1.0 - LAMBDA_INIT))
    grad = ((g - normed * jnp.mean(g * normed, axis=0, keepdims=True)) * inv_rms).astype(BF16)
    gt[...] = grad
    grad32 = grad.astype(F32)
    gn[...] = jnp.transpose(grad32).astype(BF16)
    stat1 = jnp.sum(grad32 * (ot[:, :256] * inv[0]), axis=0, keepdims=True)
    stat2 = jnp.sum(grad32 * (ot[:, 256:] * inv[1]), axis=0, keepdims=True)
    inv1 = inv[0]
    inv2 = inv[1] * lam_own

    dq[...] = jnp.zeros_like(dq)

    def backward(s, r):
        i = s * 2 + r
        dp = mm(vb[:, s, r].reshape(256, 256), gt[...])
        keys = kb[:, s, r].reshape(256, 256)
        p1 = st[0, :, i].reshape(256, 256) * inv1
        p2 = st[1, :, i].reshape(256, 256) * inv2
        mixed = (p1 - p2).astype(BF16)
        ds1 = (p1 * (dp - stat1)).astype(BF16)
        ds2 = (p2 * (dp - stat2)).astype(BF16)
        dv = mm(mixed, gn[...])
        dk1 = mm(ds1, qb[:, 0:128]) * SCALE
        dk2 = mm(ds2, qb[:, 128:256]) * -SCALE
        dq[0] += mm(keys[:, 0:128], ds1, TN)
        dq[1] += mm(keys[:, 128:256], ds2, TN)
        for part, at in ((dk1, 0), (dk2, 128), (dv, 256)):
            cols = pl.ds(at, part.shape[1])
            for t in range(2):
                piece = part[t * 128 : t * 128 + 128]
                if r:
                    sibs[s, t, :, cols] = piece.astype(BF16)
                else:
                    own[t, s, :, cols] = piece
        if r:
            send(sibs.at[s], sibr.at[s], ("sib", s), sib)

    left, right, both = pl.ds(0, 256), pl.ds(256, 256), pl.ds(0, 512)

    def total(t, s, cols):
        return own[t, s, :, cols] + sibr[s, t, :, cols].astype(F32)

    def chip_sum(t, s, cols):
        ys[t, s, :, cols] = total(t, s, cols).astype(BF16)

    def pass_on(t, s, cols, *key):
        send(ys.at[t, s, :, cols], yr.at[t, s, :, cols], ("yr", t, *key), ydev[s])

    def straight(t, s, cols, *key):
        chip_sum(t, s, cols)
        pass_on(t, s, cols, *key)

    all_sent()
    backward(2, 1)
    backward(2, 0)
    backward(1, 1)
    backward(3, 1)
    def halfway(t, up, down, *key):
        send(ys.at[t, 2, :, up], yr.at[t, 0, :, up], ("halfway", t, *key), ydev[1])
        send(ys.at[t, 2, :, down], yr.at[t, 0, :, down], ("halfway", t, *key), ydev[3])

    def second_hop(t, up, down, n):
        for s, cols in ((1, up), (3, down)):
            ys[t, s, :, cols] = (total(t, s, cols) + yr[t, 0, :, cols].astype(F32)).astype(BF16)
            pass_on(t, s, cols, n)

    groups = [(pl.ds(q * 128, 128), pl.ds(256 + q * 128, 128)) for q in range(2)]
    a_group = yr.at[1, 0, :, left]

    arrived(sibr.at[2], "sib", 2)
    chip_sum(1, 2, both)
    for q, (up, down) in enumerate(groups):
        halfway(1, up, down, q)
    backward(1, 0)
    arrived(sibr.at[1], "sib", 1)
    straight(1, 1, right, 2)
    backward(3, 0)
    arrived(sibr.at[3], "sib", 3)
    straight(1, 3, left, 2)
    chip_sum(0, 2, both)
    halfway(0, left, right)
    backward(0, 1)
    backward(0, 0)
    for j, sign in ((0, SCALE), (1, -SCALE)):
        rb[0, j * 128 : j * 128 + 128] = (dq[j, :, 0:128] * sign).astype(BF16)
        dqs[j * 128 : j * 128 + 128] = (dq[j, :, 128:256] * sign).astype(BF16)
    send(dqs, rb.at[0, pl.ds(256, 256)], ("dq",), far)
    for q, (up, down) in enumerate(groups):
        arrived(a_group, "halfway", 1, q)
        second_hop(1, up, down, q)
    straight(0, 1, right, 0)
    straight(0, 3, left, 0)
    arrived(sibr.at[0], "sib", 0)

    def finish(t, cols):
        whole = total(t, 0, cols) + (yr[t, 1, :, cols].astype(F32) + yr[t, 3, :, cols].astype(F32))
        return jnp.transpose(whole).astype(BF16)

    arrived(yr.at[0, 0], "halfway", 0)
    second_hop(0, left, right, 0)
    arrived(yr.at[1, 0], "yr", 1, 2)
    for q, group in enumerate(groups):
        arrived(a_group, "yr", 1, q)
        for cols in group:
            dks[cols, :] = finish(1, cols)
            send(dks.at[cols], rb.at[2, cols], ("dk",), far)

    blocks = [(1, 2), (1, 1), (1, 3), (0, 2), (0, 1), (0, 3), (1, 0), (0, 0)]

    def rows(r, s):
        block = lax.rem(lo + r, 2) * 4 + lax.rem(x + s, 4)
        return pl.ds(pl.multiple_of(block * 512, 512), 512)

    loaded(wb, 5)
    arrived(rb.at[0, pl.ds(256, 256)], "dq")
    for r, s in blocks:
        pa[r, s] = mm(wb[0, rows(r, s)], rb[0])
    arrived(yr.at[0, pl.ds(0, 2)], "yr", 0, 0)
    for cols in (left, right):
        rb[1, cols, :] = finish(0, cols)
    early = blocks[:2]
    for r, s in early:
        pa[r, s] += mm(wb[1, rows(r, s)], rb[1])
    arrived(rb.at[2], "dk")

    def project(r, s):
        near = 0 if (r, s) in early else mm(wb[1, rows(r, s)], rb[1])
        return pa[r, s] + (near + mm(wb[2, rows(r, s)], rb[2]))

    def top(q):
        return pl.ds(q * 256, 128)

    def bottom(q):
        return pl.ds(q * 256 + 128, 128)

    def x_first(r):
        xs_[r, 2] = project(r, 2).astype(BF16)
        for q in range(2):
            send(xs_.at[r, 2, top(q)], xr.at[r, top(q)], ("xr", r, q), xdev[1])
            send(xs_.at[r, 2, bottom(q)], xr.at[r, bottom(q)], ("xr", r, q), xdev[3])

    def x_pass(r, s, part, q):
        send(xs_.at[r, s, part], xf.at[r, s // 2, part], ("xf", r, q if r else 0), xdev[s])

    def x_direct(r):
        for q in range(2):
            for s, part in ((1, bottom(q)), (3, top(q))):
                xs_[r, s, part] = pa[r, s, part].astype(BF16)
                x_pass(r, s, part, q)

    def x_second(r, q):
        arrived(xr.at[r, pl.ds(q * 256, 256)], "xr", r, q)
        for s, part in ((1, top(q)), (3, bottom(q))):
            xs_[r, s, part] = (pa[r, s, part] + xr[r, part].astype(F32)).astype(BF16)
            x_pass(r, s, part, q)

    x_first(1)
    pa[1, 1] = project(1, 1)
    pa[1, 3] = project(1, 3)
    x_direct(1)
    x_first(0)
    for r, s in ((0, 1), (0, 3), (1, 0), (0, 0)):
        pa[r, s] = project(r, s)
    x_second(1, 0)
    x_second(1, 1)
    x_direct(0)
    x_second(0, 0)
    x_second(0, 1)
    for q in range(2):
        arrived(xf.at[0, 0], "xf", 1, q)
        part = pl.ds(q * 256, 256)
        zs[part, :] = (pa[1, 0, part] + (xf[1, 0, part].astype(F32) + xf[1, 1, part].astype(F32))).astype(BF16)
        send(zs.at[part], zr.at[part], ("zr",), partner)
    arrived(xf.at[0], "xf", 0, 0)
    ob[...] = pa[0, 0] + (xf[0, 0].astype(F32) + xf[0, 1].astype(F32))
    done = load(ob, out, 6)
    all_sent()
    done.wait()
    arrived(zr, "zr")
    assert len(names) == RECEIVES, len(names)


def body(order, qh, kh, vh, og, wq, wk, wv, wo, lam, gain):
    any_ = pl.BlockSpec(memory_space=pl.ANY)
    v = pltpu.VMEM
    parts = pl.pallas_call(
        kernel,
        out_shape=(
            jax.ShapeDtypeStruct((512, 128), F32),
            jax.ShapeDtypeStruct((512, 128), BF16),
        ),
        in_specs=[any_] * 11,
        out_specs=(any_, any_),
        scratch_shapes=[
            pltpu.SMEM((32,), jnp.int32),
            pltpu.SMEM((2,), F32),
            v((1, 256), F32),
            v((2, 4, 2, 128, 256), BF16),
            v((2, 4, 2, 128, 256), BF16),
            v((256, 256), BF16),
            v((256, 128), BF16),
            v((2, 256, 128), BF16),
            v((2, 4, 128, 512), BF16),
            v((2, 4, 512, 512), BF16),
            v((3, 4096, 512), BF16),
            v((2, 2, 8, 128, 256), F32),
            v((2, 8, 128, 512), BF16),
            v((2, 128, 256), BF16),
            v((64, 256), jnp.int32),
            v((256, 512), F32),
            v((512, 128), F32),
            v((256, 256), BF16),
            v((256, 256), BF16),
            v((2, 128, 256), F32),
            v((4, 2, 128, 512), BF16),
            v((4, 2, 128, 512), BF16),
            v((2, 4, 128, 512), F32),
            v((2, 4, 128, 512), BF16),
            v((2, 4, 128, 512), BF16),
            v((256, 128), BF16),
            v((512, 128), BF16),
            v((3, 512, 128), BF16),
            v((2, 4, 512, 128), F32),
            v((2, 4, 512, 128), BF16),
            v((2, 512, 128), BF16),
            v((2, 2, 512, 128), BF16),
            v((512, 128), BF16),
            v((512, 128), F32),
            pltpu.SemaphoreType.DMA((LOADS,)),
            pltpu.SemaphoreType.DMA((1,)),
            pltpu.SemaphoreType.DMA((RECEIVES,)),
        ],
        compiler_params=pltpu.CompilerParams(
            collective_id=0, has_side_effects=True, vmem_limit_bytes=56 * 2**20
        ),
        name="differential_attention_backward",
    )(order, lam, gain.reshape(1, 256), qh, kh, vh, og, wq, wk, wv, wo)
    return parts[0] + parts[1].astype(F32)


def solution(mesh):
    in_specs = (
        P(),
        P("ctx", "heads"),
        P("ctx", "heads"),
        P("ctx", "heads"),
        P("ctx", "heads"),
        P(None, "heads"),
        P(None, "heads"),
        P(None, "heads"),
        P("heads", None),
        P("heads"),
        P(),
    )
    out_specs = P("heads", "ctx")
    return jax.shard_map(body, mesh=mesh, in_specs=in_specs, out_specs=out_specs, check_vma=False)
```

```python
import math

import jax
import jax.numpy as jnp
from jax import lax
from jax.experimental import pallas as pl
from jax.experimental.pallas import tpu as pltpu
from jax.sharding import PartitionSpec as P

MESH = pl.DeviceIdType.MESH
HDIM = 128
WIDTH = 256
LAMBDA_INIT = 0.8
EPSILON = 1e-05
MASKED = -1e30
SCALE = HDIM**-0.5
LOG2E = 1.4426950408889634
F32 = jnp.float32
BF16 = jnp.bfloat16


def mm(a, b, dims=((1,), (0,))):
    return lax.dot_general(a, b, (dims, ((), ())), preferred_element_type=F32)


RECEIVES = 46
LOADS = 7
NT = ((1,), (1,))
TN = ((0,), (0,))


def kernel(
    order_in, lam_in, gain_in, qh, kh, vh, og, wq, wk, wv, wo, out, zr,
    order, lam, gain, kb, vb, qb, gs, gb, ogb, wob, wb, st, pb, qt, d0, ot, gacc, gt, gn, dq,
    sibs, sibr, own, ys, yr, dqs, dks, rb, pa, xs_, xr, xf, zs, ob,
    lsem, ssem, rsem,
):
    ctx = lax.axis_index("ctx")
    hd = lax.axis_index("heads")
    hi = lax.div(ctx, 8)
    y = lax.rem(lax.div(ctx, 2), 4)
    c = lax.rem(ctx, 2)
    lo = lax.div(hd, 4)
    x = lax.rem(hd, 4)

    def dev(hi_, y_, c_, lo_, x_):
        return (hi_ * 8 + y_ * 2 + c_, lo_ * 4 + x_)

    sib = dev(hi, y, 1 - c, lo, x)
    ydev = {s: dev(hi, lax.rem(y + s, 4), c, lo, x) for s in (1, 2, 3)}
    xdev = {s: dev(hi, y, c, lo, lax.rem(x + s, 4)) for s in (1, 2, 3)}
    far = dev(1 - hi, y, c, lo, x)
    partner = dev(hi, y, c, 1 - lo, x)

    barrier = pltpu.get_barrier_semaphore()
    others = [sib, far, partner, *ydev.values(), *xdev.values()]
    for d in others:
        pl.semaphore_signal(barrier, inc=1, device_id=d, device_id_type=MESH)

    def half(rel):
        head = hi if rel == 0 else 1 - hi
        return pl.ds(pl.multiple_of(head * 256, 256), 256)

    def load(src, dst, n):
        cp = pltpu.make_async_copy(src, dst, lsem.at[n])
        cp.start()
        return cp

    small = [load(order_in, order, 0), load(lam_in, lam, 1), load(gain_in, gain, 2)]
    load(kh.at[:, half(0)], kb.at[0, 0, 0], 3)
    load(vh.at[:, half(0)], vb.at[0, 0, 0], 3)
    load(qh.at[:, half(0)], qb.at[pl.ds(0, 128)], 3)
    load(og, ogb.at[0, 0], 3)

    def loaded(ref, n):
        pltpu.make_async_copy(ref, ref, lsem.at[n]).wait()

    pl.semaphore_wait(barrier, len(others))

    names = {}
    sent = [0]

    def num(*key):
        if key not in names:
            names[key] = len(names)
        return names[key]

    def send(src, dst, key, to):
        pltpu.make_async_remote_copy(
            src_ref=src, dst_ref=dst, send_sem=ssem.at[0], recv_sem=rsem.at[num(*key)],
            device_id=to, device_id_type=MESH,
        ).start()
        sent[0] += math.prod(src.shape) * src.dtype.itemsize

    def all_sent():
        rows = wb.at[0, pl.ds(0, sent[0] // 1024)]
        pltpu.make_async_remote_copy(
            src_ref=rows, dst_ref=rows, send_sem=ssem.at[0], recv_sem=rsem.at[0],
            device_id=sib, device_id_type=MESH,
        ).wait_send()
        sent[0] = 0

    def arrived(dst, *key):
        pltpu.make_async_remote_copy(
            src_ref=dst, dst_ref=dst, send_sem=ssem.at[0], recv_sem=rsem.at[num(*key)],
            device_id=sib, device_id_type=MESH,
        ).wait_recv()

    def gather_y(src, buf, key, t, steps=(2, 3, 1)):
        for s in steps:
            send(src, buf.at[t, s, 0], (*key, s) if len(key) > 1 else key, ydev[4 - s])

    def twin(buf, s, t, *key):
        send(buf.at[t, s, 0], buf.at[t, s, 1], key, sib)

    def gather_x(src, r, steps=(2, 3, 1)):
        for s in steps:
            send(src, ogb.at[r, s], ("og", r, s == 2), xdev[4 - s])

    send(kh.at[:, half(1)], kb.at[1, 0, 0], ("k far",), far)
    send(og, ogb.at[1, 0], ("og partner",), partner)
    gather_y(kh.at[:, half(0)], kb, ("k0",), 0)
    gather_x(og, 0)
    send(vh.at[:, half(1)], vb.at[1, 0, 0], ("v far",), far)
    gather_y(vh.at[:, half(0)], vb, ("v0",), 0, (3, 1))
    send(qh.at[:, half(1)], qb.at[pl.ds(128, 128)], ("q",), far)
    send(kh.at[:, half(0)], kb.at[0, 0, 1], ("k0 twin",), sib)
    send(vh.at[:, half(0)], vb.at[0, 0, 1], ("v0 twin",), sib)

    for cp in small:
        cp.wait()
    lane = lax.broadcasted_iota(jnp.int32, (64, 256), 1)
    row = lax.broadcasted_iota(jnp.int32, (64, 256), 0)

    def stretch(s, r, t, piece):
        token_half = hi if t == 0 else 1 - hi
        block = token_half * 8 + lax.rem(y + s, 4) * 2 + lax.rem(c + r, 2)
        return order[block * 2 + piece]

    qs = [stretch(0, 0, t, piece) for t in range(2) for piece in range(2)]
    qstretch = jnp.where(
        lane < 128,
        jnp.where(lane < 64, qs[0], qs[1]),
        jnp.where(lane < 192, qs[2], qs[3]),
    )
    d0[...] = row - qstretch * 64 - lax.rem(lane, 64)

    def scores(s, t, peak):
        peaks = list(peak)
        for j in range(2):
            keys = kb[t, s].reshape(256, 256)[:, j * 128 : j * 128 + 128]
            sc = mm(keys, qt[j]) * (SCALE * LOG2E)
            for n in range(4):
                threshold = stretch(s, n // 2, t, n % 2) * -64
                part = jnp.where(d0[...] <= threshold, sc[n * 64 : n * 64 + 64], MASKED)
                at = pl.ds(n % 2 * 64, 64)
                st[j, t, s * 2 + n // 2, at] = part
                peaks[j] = jnp.maximum(peaks[j], jnp.max(part.reshape(8, 8, 256), axis=0))
        return tuple(peaks)

    def gdot(r, s, head=None, start=False):
        rows = pl.ds(0, 512) if head is None else half(head)
        term = mm(wob[r, s, rows], ogb[r, s], NT)
        gacc[rows] = term if start else gacc[rows] + term

    for s in range(4):
        for r in range(2):
            block = lax.rem(lo + r, 2) * 4 + lax.rem(x + s, 4)
            at = pl.ds(pl.multiple_of(block * 512, 512), 512)
            load(wo.at[:, at], wob.at[r, s], 4)
    arrived(kb.at[1, 0, 0], "k far")
    gather_y(kb.at[1, 0, 0], kb, ("k1",), 1)
    twin(kb, 0, 1, "k1 twin")
    arrived(ogb.at[1, 0], "og partner")
    gather_x(ogb.at[1, 0], 1, (3, 1))
    arrived(ogb.at[0, 2], "og", 0, True)
    send(ogb.at[0, 2], ogb.at[1, 2], ("og", 1, True), partner)
    arrived(kb.at[0, pl.ds(1, 3), 0], "k0")
    for s in (1, 3, 2):
        twin(kb, s, 0, "k0 twin")
    lower, upper = pl.ds(0, 64), pl.ds(64, 64)
    arrived(vb.at[0, pl.ds(1, 2), 0], "v0")
    for s, part, to in ((3, lower, 1), (1, upper, 3)):
        send(vb.at[0, s, 0, part], vb.at[0, 2, 0, part], ("v0 relay",), ydev[to])
        twin(vb, s, 0, "v0 twin")
    for w, rel, group, at in (
        (wq, 0, 0, 0), (wq, 1, 0, 256), (wk, 0, 1, 0), (wv, 0, 1, 256), (wk, 1, 2, 0), (wv, 1, 2, 256),
    ):
        load(w.at[:, half(rel)], wb.at[group, :, pl.ds(at, 256)], 5)
    loaded(wb.at[0, pl.ds(0, 320)], 3)
    loaded(wob, 4)
    gdot(0, 0, start=True)
    gdot(1, 0)
    gdot(0, 2)
    arrived(vb.at[1, 0, 0], "v far")
    gather_y(vb.at[1, 0, 0], vb, ("v1", "y"), 1)
    twin(vb, 0, 1, "v1 twin", 0)
    arrived(ogb.at[0, pl.ds(0, 2)], "og", 0, False)
    gdot(0, 1)
    gdot(0, 3)
    arrived(qb.at[pl.ds(128, 128)], "q")
    for j in range(2):
        qt[j] = jnp.transpose(qb[:, j * 128 : j * 128 + 128].astype(F32)).astype(BF16)
    peak = (jnp.full((8, 256), MASKED, F32),) * 2
    arrived(kb.at[0, :, 1], "k0 twin")
    for s in (0, 1):
        peak = scores(s, 0, peak)
    arrived(kb.at[1, pl.ds(1, 3), 0], "k1")
    for s in (1, 3, 2):
        twin(kb, s, 1, "k1 twin")
    arrived(vb.at[0, 2, 0], "v0 relay")
    twin(vb, 2, 0, "v0 twin")
    arrived(ogb.at[1, pl.ds(0, 2)], "og", 1, False)
    gdot(1, 1, 1)
    gdot(1, 3, 1)
    arrived(ogb.at[1, 2], "og", 1, True)
    gdot(1, 2, 1)
    gs[...] = gacc[half(1)].astype(BF16)
    send(gs, gb.at[1], ("g",), far)
    for s in (1, 3, 2):
        gdot(1, s, 0)
    gb[0] = gacc[half(0)].astype(BF16)
    for s in (3, 2):
        peak = scores(s, 0, peak)

    def weigh(t, tops):
        def step(i, sums):
            sums = list(sums)
            for j in range(2):
                p = jnp.exp2(st[j, t, i] - tops[j])
                st[j, t, i] = p
                sums[j] = sums[j] + jnp.sum(p.reshape(16, 8, 256), axis=0)
                pb[t, i, :, j * 256 : j * 256 + 256] = p.astype(BF16)
            return tuple(sums)

        sums = lax.fori_loop(0, 8, step, (jnp.zeros((8, 256), F32),) * 2, unroll=2)
        return [jnp.sum(p, axis=0, keepdims=True) for p in sums]

    tops0 = [jnp.max(p, axis=0, keepdims=True) for p in peak]
    sums0 = weigh(0, tops0)
    arrived(vb.at[0, :, 1], "v0 twin")
    ot[...] = mm(vb[0].reshape(1024, 256), pb[0].reshape(1024, 512), TN)
    for s in (1, 3):
        arrived(vb.at[1, s, 0], "v1", "y", s)
        twin(vb, s, 1, "v1 twin", 0)
    arrived(kb.at[1, :, 1], "k1 twin")
    for s in range(4):
        peak = scores(s, 1, peak)

    arrived(vb.at[1, 2, 0], "v1", "y", 2)
    twin(vb, 2, 1, "v1 twin", 1)
    tops = [jnp.max(p, axis=0, keepdims=True) for p in peak]
    scales = [jnp.exp2(t0 - t1) for t0, t1 in zip(tops0, tops)]
    sums1 = weigh(1, tops)
    inv = [1.0 / (n * f + m) for n, f, m in zip(sums0, scales, sums1)]

    def values(t, s):
        return mm(vb[t, s].reshape(256, 256), pb[t, 2 * s : 2 * s + 2].reshape(256, 512), TN)

    ot[...] = ot[...] * jnp.concatenate(scales, axis=1)
    arrived(vb.at[1, pl.ds(0, 3), 1], "v1 twin", 0)
    for s in (0, 1, 3):
        ot[...] += values(1, s)
    arrived(vb.at[1, 2, 1], "v1 twin", 1)
    ot[...] += values(1, 2)

    lam_own = lam[hi]
    gain_t = jnp.transpose(jnp.broadcast_to(gain[...], (128, 256)))
    gain_t = jnp.concatenate([gain_t, gain_t], axis=1)
    arrived(gb.at[1], "g")

    o1 = ot[:, :256] * inv[0]
    o2 = ot[:, 256:] * inv[1]
    combined = o1 - lam_own * o2
    rms = jnp.sqrt(jnp.mean(combined * combined, axis=0, keepdims=True) + EPSILON)
    inv_rms = 1.0 / rms
    normed = combined * inv_rms
    g = jnp.concatenate([gb[0], gb[1]], axis=1).astype(F32) * (gain_t * (1.0 - LAMBDA_INIT))
    grad = ((g - normed * jnp.mean(g * normed, axis=0, keepdims=True)) * inv_rms).astype(BF16)
    gt[...] = grad
    grad32 = grad.astype(F32)
    gn[...] = jnp.transpose(grad32).astype(BF16)
    stat1 = jnp.sum(grad32 * (ot[:, :256] * inv[0]), axis=0, keepdims=True)
    stat2 = jnp.sum(grad32 * (ot[:, 256:] * inv[1]), axis=0, keepdims=True)
    inv1 = inv[0]
    inv2 = inv[1] * lam_own

    dq[...] = jnp.zeros_like(dq)

    def backward(s, r):
        i = s * 2 + r
        dp = mm(vb[:, s, r].reshape(256, 256), gt[...])
        keys = kb[:, s, r].reshape(256, 256)
        p1 = jnp.concatenate([st[0, 0, i] * (inv1 * scales[0]), st[0, 1, i] * inv1], axis=0)
        p2 = jnp.concatenate([st[1, 0, i] * (inv2 * scales[1]), st[1, 1, i] * inv2], axis=0)
        mixed = (p1 - p2).astype(BF16)
        ds1 = (p1 * (dp - stat1)).astype(BF16)
        ds2 = (p2 * (dp - stat2)).astype(BF16)
        dv = mm(mixed, gn[...])
        dk1 = mm(ds1, qb[:, 0:128]) * SCALE
        dk2 = mm(ds2, qb[:, 128:256]) * -SCALE
        dq[0] += mm(keys[:, 0:128], ds1, TN)
        dq[1] += mm(keys[:, 128:256], ds2, TN)
        for part, at in ((dk1, 0), (dk2, 128), (dv, 256)):
            cols = pl.ds(at, part.shape[1])
            for t in range(2):
                piece = part[t * 128 : t * 128 + 128]
                if r:
                    sibs[s, t, :, cols] = piece.astype(BF16)
                else:
                    own[t, s, :, cols] = piece
        if r:
            send(sibs.at[s], sibr.at[s], ("sib", s), sib)

    left, right, both = pl.ds(0, 256), pl.ds(256, 256), pl.ds(0, 512)

    def total(t, s, cols):
        return own[t, s, :, cols] + sibr[s, t, :, cols].astype(F32)

    def chip_sum(t, s, cols):
        ys[t, s, :, cols] = total(t, s, cols).astype(BF16)

    def pass_on(t, s, cols, *key):
        send(ys.at[t, s, :, cols], yr.at[t, s, :, cols], ("yr", t, *key), ydev[s])

    def straight(t, s, cols, *key):
        chip_sum(t, s, cols)
        pass_on(t, s, cols, *key)

    all_sent()
    backward(2, 1)
    backward(2, 0)
    backward(1, 1)
    def halfway(t, up, down, *key):
        send(ys.at[t, 2, :, up], yr.at[t, 0, :, up], ("halfway", t, *key), ydev[1])
        send(ys.at[t, 2, :, down], yr.at[t, 0, :, down], ("halfway", t, *key), ydev[3])

    def second_hop(t, up, down, n):
        for s, cols in ((1, up), (3, down)):
            ys[t, s, :, cols] = (total(t, s, cols) + yr[t, 0, :, cols].astype(F32)).astype(BF16)
            pass_on(t, s, cols, n)

    groups = [(pl.ds(q * 128, 128), pl.ds(256 + q * 128, 128)) for q in range(2)]
    a_group = yr.at[1, 0, :, left]

    arrived(sibr.at[2], "sib", 2)
    chip_sum(1, 2, both)
    for q, (up, down) in enumerate(groups):
        halfway(1, up, down, q)
    backward(3, 1)
    backward(1, 0)
    arrived(sibr.at[1], "sib", 1)
    straight(1, 1, right, 2)
    backward(3, 0)
    arrived(sibr.at[3], "sib", 3)
    straight(1, 3, left, 2)
    chip_sum(0, 2, both)
    halfway(0, left, right)
    backward(0, 1)
    backward(0, 0)
    for j, sign in ((0, SCALE), (1, -SCALE)):
        rb[0, j * 128 : j * 128 + 128] = (dq[j, :, 0:128] * sign).astype(BF16)
        dqs[j * 128 : j * 128 + 128] = (dq[j, :, 128:256] * sign).astype(BF16)
    send(dqs, rb.at[0, pl.ds(256, 256)], ("dq",), far)
    for q, (up, down) in enumerate(groups):
        arrived(a_group, "halfway", 1, q)
        second_hop(1, up, down, q)
    straight(0, 1, right, 0)
    straight(0, 3, left, 0)
    arrived(sibr.at[0], "sib", 0)

    def finish(t, cols):
        whole = total(t, 0, cols) + (yr[t, 1, :, cols].astype(F32) + yr[t, 3, :, cols].astype(F32))
        return jnp.transpose(whole).astype(BF16)

    arrived(yr.at[0, 0], "halfway", 0)
    second_hop(0, left, right, 0)
    arrived(yr.at[1, 0], "yr", 1, 2)
    for q, group in enumerate(groups):
        arrived(a_group, "yr", 1, q)
        for cols in group:
            dks[cols, :] = finish(1, cols)
            send(dks.at[cols], rb.at[2, cols], ("dk",), far)

    blocks = [(1, 2), (1, 1), (1, 3), (0, 2), (0, 1), (0, 3), (1, 0), (0, 0)]

    def rows(r, s):
        block = lax.rem(lo + r, 2) * 4 + lax.rem(x + s, 4)
        return pl.ds(pl.multiple_of(block * 512, 512), 512)

    loaded(wb, 5)
    arrived(rb.at[0, pl.ds(256, 256)], "dq")
    for r, s in blocks:
        pa[r, s] = mm(wb[0, rows(r, s)], rb[0])
    arrived(yr.at[0, pl.ds(0, 2)], "yr", 0, 0)
    for cols in (left, right):
        rb[1, cols, :] = finish(0, cols)
    early = blocks[:2]
    for r, s in early:
        pa[r, s] += mm(wb[1, rows(r, s)], rb[1])
    arrived(rb.at[2], "dk")

    def project(r, s):
        near = 0 if (r, s) in early else mm(wb[1, rows(r, s)], rb[1])
        return pa[r, s] + (near + mm(wb[2, rows(r, s)], rb[2]))

    pieces = (2, 4)

    def features(r, q):
        return pl.ds(q * (512 // pieces[r]), 512 // pieces[r])

    def top(r, q):
        return pl.ds(q * (512 // pieces[r]), 256 // pieces[r])

    def bottom(r, q):
        return pl.ds(q * (512 // pieces[r]) + 256 // pieces[r], 256 // pieces[r])

    def x_first(r):
        xs_[r, 2] = project(r, 2).astype(BF16)
        for q in range(pieces[r]):
            send(xs_.at[r, 2, top(r, q)], xr.at[r, top(r, q)], ("xr", r, q), xdev[1])
            send(xs_.at[r, 2, bottom(r, q)], xr.at[r, bottom(r, q)], ("xr", r, q), xdev[3])

    def x_pass(r, s, part, q):
        send(xs_.at[r, s, part], xf.at[r, s // 2, part], ("xf", r, q if r else 0), xdev[s])

    def x_direct(r):
        for q in range(pieces[r]):
            for s, part in ((1, bottom(r, q)), (3, top(r, q))):
                xs_[r, s, part] = pa[r, s, part].astype(BF16)
                x_pass(r, s, part, q)

    def x_second(r, q):
        arrived(xr.at[r, features(r, q)], "xr", r, q)
        for s, part in ((1, top(r, q)), (3, bottom(r, q))):
            xs_[r, s, part] = (pa[r, s, part] + xr[r, part].astype(F32)).astype(BF16)
            x_pass(r, s, part, q)

    x_first(1)
    pa[1, 1] = project(1, 1)
    pa[1, 3] = project(1, 3)
    x_direct(1)
    x_first(0)
    for r, s in ((0, 1), (0, 3), (1, 0), (0, 0)):
        pa[r, s] = project(r, s)
    for q in range(pieces[1]):
        x_second(1, q)
    x_direct(0)
    for q in range(pieces[0]):
        x_second(0, q)
    for q in range(pieces[1]):
        part = features(1, q)
        arrived(xf.at[1, :, part], "xf", 1, q)
        zs[part, :] = (pa[1, 0, part] + (xf[1, 0, part].astype(F32) + xf[1, 1, part].astype(F32))).astype(BF16)
        send(zs.at[part], zr.at[part], ("zr",), partner)
    arrived(xf.at[0], "xf", 0, 0)
    ob[...] = pa[0, 0] + (xf[0, 0].astype(F32) + xf[0, 1].astype(F32))
    done = load(ob, out, 6)
    all_sent()
    done.wait()
    arrived(zr, "zr")
    assert len(names) == RECEIVES, len(names)


def body(order, qh, kh, vh, og, wq, wk, wv, wo, lam, gain):
    any_ = pl.BlockSpec(memory_space=pl.ANY)
    v = pltpu.VMEM
    parts = pl.pallas_call(
        kernel,
        out_shape=(
            jax.ShapeDtypeStruct((512, 128), F32),
            jax.ShapeDtypeStruct((512, 128), BF16),
        ),
        in_specs=[any_] * 11,
        out_specs=(any_, any_),
        scratch_shapes=[
            pltpu.SMEM((32,), jnp.int32),
            pltpu.SMEM((2,), F32),
            v((1, 256), F32),
            v((2, 4, 2, 128, 256), BF16),
            v((2, 4, 2, 128, 256), BF16),
            v((256, 256), BF16),
            v((256, 128), BF16),
            v((2, 256, 128), BF16),
            v((2, 4, 128, 512), BF16),
            v((2, 4, 512, 512), BF16),
            v((3, 4096, 512), BF16),
            v((2, 2, 8, 128, 256), F32),
            v((2, 8, 128, 512), BF16),
            v((2, 128, 256), BF16),
            v((64, 256), jnp.int32),
            v((256, 512), F32),
            v((512, 128), F32),
            v((256, 256), BF16),
            v((256, 256), BF16),
            v((2, 128, 256), F32),
            v((4, 2, 128, 512), BF16),
            v((4, 2, 128, 512), BF16),
            v((2, 4, 128, 512), F32),
            v((2, 4, 128, 512), BF16),
            v((2, 4, 128, 512), BF16),
            v((256, 128), BF16),
            v((512, 128), BF16),
            v((3, 512, 128), BF16),
            v((2, 4, 512, 128), F32),
            v((2, 4, 512, 128), BF16),
            v((2, 512, 128), BF16),
            v((2, 2, 512, 128), BF16),
            v((512, 128), BF16),
            v((512, 128), F32),
            pltpu.SemaphoreType.DMA((LOADS,)),
            pltpu.SemaphoreType.DMA((1,)),
            pltpu.SemaphoreType.DMA((RECEIVES,)),
        ],
        compiler_params=pltpu.CompilerParams(
            collective_id=0, has_side_effects=True, vmem_limit_bytes=56 * 2**20
        ),
        name="differential_attention_backward",
    )(order, lam, gain.reshape(1, 256), qh, kh, vh, og, wq, wk, wv, wo)
    return parts[0] + parts[1].astype(F32)


def solution(mesh):
    in_specs = (
        P(),
        P("ctx", "heads"),
        P("ctx", "heads"),
        P("ctx", "heads"),
        P("ctx", "heads"),
        P(None, "heads"),
        P(None, "heads"),
        P(None, "heads"),
        P("heads", None),
        P("heads"),
        P(),
    )
    out_specs = P("heads", "ctx")
    return jax.shard_map(body, mesh=mesh, in_specs=in_specs, out_specs=out_specs, check_vma=False)
```

```python
import math

import jax
import jax.numpy as jnp
from jax import lax
from jax.experimental import pallas as pl
from jax.experimental.pallas import tpu as pltpu
from jax.sharding import PartitionSpec as P

MESH = pl.DeviceIdType.MESH
HDIM = 128
WIDTH = 256
LAMBDA_INIT = 0.8
EPSILON = 1e-05
MASKED = -1e30
SCALE = HDIM**-0.5
LOG2E = 1.4426950408889634
F32 = jnp.float32
BF16 = jnp.bfloat16


def mm(a, b, dims=((1,), (0,))):
    return lax.dot_general(a, b, (dims, ((), ())), preferred_element_type=F32)


RECEIVES = 48
LOADS = 7
NT = ((1,), (1,))
TN = ((0,), (0,))


def kernel(
    order_in, lam_in, gain_in, qh, kh, vh, og, wq, wk, wv, wo, out, zr,
    order, lam, gain, kb, vb, qb, gs, gb, ogb, wob, wb, st, pb, qt, d0, ot, gacc, gt, gn, dq,
    sibs, sibr, own, ys, yr, dqs, dks, rb, pa, xs_, xr, xf, zs, ob,
    lsem, ssem, rsem,
):
    ctx = lax.axis_index("ctx")
    hd = lax.axis_index("heads")
    hi = lax.div(ctx, 8)
    y = lax.rem(lax.div(ctx, 2), 4)
    c = lax.rem(ctx, 2)
    lo = lax.div(hd, 4)
    x = lax.rem(hd, 4)

    def dev(hi_, y_, c_, lo_, x_):
        return (hi_ * 8 + y_ * 2 + c_, lo_ * 4 + x_)

    sib = dev(hi, y, 1 - c, lo, x)
    ydev = {s: dev(hi, lax.rem(y + s, 4), c, lo, x) for s in (1, 2, 3)}
    xdev = {s: dev(hi, y, c, lo, lax.rem(x + s, 4)) for s in (1, 2, 3)}
    far = dev(1 - hi, y, c, lo, x)
    partner = dev(hi, y, c, 1 - lo, x)

    barrier = pltpu.get_barrier_semaphore()
    others = [sib, far, partner, *ydev.values(), *xdev.values()]
    for d in others:
        pl.semaphore_signal(barrier, inc=1, device_id=d, device_id_type=MESH)

    def half(rel):
        head = hi if rel == 0 else 1 - hi
        return pl.ds(pl.multiple_of(head * 256, 256), 256)

    def load(src, dst, n):
        cp = pltpu.make_async_copy(src, dst, lsem.at[n])
        cp.start()
        return cp

    small = [load(order_in, order, 0), load(lam_in, lam, 1), load(gain_in, gain, 2)]
    load(kh.at[:, half(0)], kb.at[0, 0, 0], 3)
    load(vh.at[:, half(0)], vb.at[0, 0, 0], 3)
    load(qh.at[:, half(0)], qb.at[pl.ds(0, 128)], 3)
    load(og, ogb.at[0, 0], 3)

    def loaded(ref, n):
        pltpu.make_async_copy(ref, ref, lsem.at[n]).wait()

    pl.semaphore_wait(barrier, len(others))

    names = {}
    sent = [0]

    def num(*key):
        if key not in names:
            names[key] = len(names)
        return names[key]

    def send(src, dst, key, to):
        pltpu.make_async_remote_copy(
            src_ref=src, dst_ref=dst, send_sem=ssem.at[0], recv_sem=rsem.at[num(*key)],
            device_id=to, device_id_type=MESH,
        ).start()
        sent[0] += math.prod(src.shape) * src.dtype.itemsize

    def all_sent():
        rows = wb.at[0, pl.ds(0, sent[0] // 1024)]
        pltpu.make_async_remote_copy(
            src_ref=rows, dst_ref=rows, send_sem=ssem.at[0], recv_sem=rsem.at[0],
            device_id=sib, device_id_type=MESH,
        ).wait_send()
        sent[0] = 0

    def arrived(dst, *key):
        pltpu.make_async_remote_copy(
            src_ref=dst, dst_ref=dst, send_sem=ssem.at[0], recv_sem=rsem.at[num(*key)],
            device_id=sib, device_id_type=MESH,
        ).wait_recv()

    def gather_y(src, buf, key, t, steps=(2, 3, 1)):
        for s in steps:
            send(src, buf.at[t, s, 0], (*key, s) if len(key) > 1 else key, ydev[4 - s])

    def twin(buf, s, t, *key):
        send(buf.at[t, s, 0], buf.at[t, s, 1], key, sib)

    def gather_x(src, r, steps=(2, 3, 1)):
        for s in steps:
            send(src, ogb.at[r, s], ("og", r, s == 2), xdev[4 - s])

    send(kh.at[:, half(1)], kb.at[1, 0, 0], ("k far",), far)
    send(og, ogb.at[1, 0], ("og partner",), partner)
    gather_y(kh.at[:, half(0)], kb, ("k0",), 0)
    gather_x(og, 0)
    send(vh.at[:, half(1)], vb.at[1, 0, 0], ("v far",), far)
    gather_y(vh.at[:, half(0)], vb, ("v0",), 0, (3, 1))
    send(qh.at[:, half(1)], qb.at[pl.ds(128, 128)], ("q",), far)
    send(kh.at[:, half(0)], kb.at[0, 0, 1], ("k0 twin",), sib)
    send(vh.at[:, half(0)], vb.at[0, 0, 1], ("v0 twin",), sib)

    for cp in small:
        cp.wait()
    lane = lax.broadcasted_iota(jnp.int32, (64, 256), 1)
    row = lax.broadcasted_iota(jnp.int32, (64, 256), 0)

    def stretch(s, r, t, piece):
        token_half = hi if t == 0 else 1 - hi
        block = token_half * 8 + lax.rem(y + s, 4) * 2 + lax.rem(c + r, 2)
        return order[block * 2 + piece]

    qs = [stretch(0, 0, t, piece) for t in range(2) for piece in range(2)]
    qstretch = jnp.where(
        lane < 128,
        jnp.where(lane < 64, qs[0], qs[1]),
        jnp.where(lane < 192, qs[2], qs[3]),
    )
    d0[...] = row - qstretch * 64 - lax.rem(lane, 64)

    def scores(s, t, peak):
        peaks = list(peak)
        for j in range(2):
            keys = kb[t, s].reshape(256, 256)[:, j * 128 : j * 128 + 128]
            sc = mm(keys, qt[j]) * (SCALE * LOG2E)
            for n in range(4):
                threshold = stretch(s, n // 2, t, n % 2) * -64
                part = jnp.where(d0[...] <= threshold, sc[n * 64 : n * 64 + 64], MASKED)
                at = pl.ds(n % 2 * 64, 64)
                st[j, t, s * 2 + n // 2, at] = part
                peaks[j] = jnp.maximum(peaks[j], jnp.max(part.reshape(8, 8, 256), axis=0))
        return tuple(peaks)

    def gdot(r, s, head=None, start=False):
        rows = pl.ds(0, 512) if head is None else half(head)
        term = mm(wob[r, s, rows], ogb[r, s], NT)
        gacc[rows] = term if start else gacc[rows] + term

    for s in range(4):
        for r in range(2):
            block = lax.rem(lo + r, 2) * 4 + lax.rem(x + s, 4)
            at = pl.ds(pl.multiple_of(block * 512, 512), 512)
            load(wo.at[:, at], wob.at[r, s], 4)
    arrived(kb.at[1, 0, 0], "k far")
    gather_y(kb.at[1, 0, 0], kb, ("k1",), 1)
    twin(kb, 0, 1, "k1 twin")
    arrived(ogb.at[1, 0], "og partner")
    gather_x(ogb.at[1, 0], 1, (3, 1))
    arrived(ogb.at[0, 2], "og", 0, True)
    send(ogb.at[0, 2], ogb.at[1, 2], ("og", 1, True), partner)
    arrived(kb.at[0, pl.ds(1, 3), 0], "k0")
    for s in (1, 3, 2):
        twin(kb, s, 0, "k0 twin")
    lower, upper = pl.ds(0, 64), pl.ds(64, 64)
    arrived(vb.at[0, pl.ds(1, 2), 0], "v0")
    for s, part, to in ((3, lower, 1), (1, upper, 3)):
        send(vb.at[0, s, 0, part], vb.at[0, 2, 0, part], ("v0 relay",), ydev[to])
        twin(vb, s, 0, "v0 twin")
    for w, rel, group, at in (
        (wq, 0, 0, 0), (wq, 1, 0, 256), (wk, 0, 1, 0), (wv, 0, 1, 256), (wk, 1, 2, 0), (wv, 1, 2, 256),
    ):
        load(w.at[:, half(rel)], wb.at[group, :, pl.ds(at, 256)], 5)
    loaded(wb.at[0, pl.ds(0, 320)], 3)
    loaded(wob, 4)
    gdot(0, 0, start=True)
    gdot(1, 0)
    gdot(0, 2)
    arrived(vb.at[1, 0, 0], "v far")
    gather_y(vb.at[1, 0, 0], vb, ("v1", "y"), 1)
    twin(vb, 0, 1, "v1 twin", 0)
    arrived(ogb.at[0, pl.ds(0, 2)], "og", 0, False)
    gdot(0, 1)
    gdot(0, 3)
    arrived(qb.at[pl.ds(128, 128)], "q")
    for j in range(2):
        qt[j] = jnp.transpose(qb[:, j * 128 : j * 128 + 128].astype(F32)).astype(BF16)
    peak = (jnp.full((8, 256), MASKED, F32),) * 2
    arrived(kb.at[0, :, 1], "k0 twin")
    for s in (0, 1):
        peak = scores(s, 0, peak)
    arrived(kb.at[1, pl.ds(1, 3), 0], "k1")
    for s in (1, 3, 2):
        twin(kb, s, 1, "k1 twin")
    arrived(vb.at[0, 2, 0], "v0 relay")
    twin(vb, 2, 0, "v0 twin")
    arrived(ogb.at[1, pl.ds(0, 2)], "og", 1, False)
    gdot(1, 1, 1)
    gdot(1, 3, 1)
    arrived(ogb.at[1, 2], "og", 1, True)
    gdot(1, 2, 1)
    gs[...] = gacc[half(1)].astype(BF16)
    send(gs, gb.at[1], ("g",), far)
    for s in (1, 3, 2):
        gdot(1, s, 0)
    gb[0] = gacc[half(0)].astype(BF16)
    for s in (3, 2):
        peak = scores(s, 0, peak)

    def weigh(t, tops):
        def step(i, sums):
            sums = list(sums)
            for j in range(2):
                p = jnp.exp2(st[j, t, i] - tops[j])
                st[j, t, i] = p
                sums[j] = sums[j] + jnp.sum(p.reshape(16, 8, 256), axis=0)
                pb[t, i, :, j * 256 : j * 256 + 256] = p.astype(BF16)
            return tuple(sums)

        sums = lax.fori_loop(0, 8, step, (jnp.zeros((8, 256), F32),) * 2, unroll=2)
        return [jnp.sum(p, axis=0, keepdims=True) for p in sums]

    tops0 = [jnp.max(p, axis=0, keepdims=True) for p in peak]
    sums0 = weigh(0, tops0)
    arrived(vb.at[0, :, 1], "v0 twin")
    ot[...] = mm(vb[0].reshape(1024, 256), pb[0].reshape(1024, 512), TN)
    for s in (1, 3):
        arrived(vb.at[1, s, 0], "v1", "y", s)
        twin(vb, s, 1, "v1 twin", 0)
    arrived(kb.at[1, :, 1], "k1 twin")
    for s in range(4):
        peak = scores(s, 1, peak)

    arrived(vb.at[1, 2, 0], "v1", "y", 2)
    twin(vb, 2, 1, "v1 twin", 1)
    tops = [jnp.max(p, axis=0, keepdims=True) for p in peak]
    scales = [jnp.exp2(t0 - t1) for t0, t1 in zip(tops0, tops)]
    sums1 = weigh(1, tops)
    inv = [1.0 / (n * f + m) for n, f, m in zip(sums0, scales, sums1)]

    def values(t, s):
        return mm(vb[t, s].reshape(256, 256), pb[t, 2 * s : 2 * s + 2].reshape(256, 512), TN)

    ot[...] = ot[...] * jnp.concatenate(scales, axis=1)
    arrived(vb.at[1, pl.ds(0, 3), 1], "v1 twin", 0)
    for s in (0, 1, 3):
        ot[...] += values(1, s)
    arrived(vb.at[1, 2, 1], "v1 twin", 1)
    ot[...] += values(1, 2)

    lam_own = lam[hi]
    gain_t = jnp.transpose(jnp.broadcast_to(gain[...], (128, 256)))
    gain_t = jnp.concatenate([gain_t, gain_t], axis=1)
    arrived(gb.at[1], "g")

    o1 = ot[:, :256] * inv[0]
    o2 = ot[:, 256:] * inv[1]
    combined = o1 - lam_own * o2
    rms = jnp.sqrt(jnp.mean(combined * combined, axis=0, keepdims=True) + EPSILON)
    inv_rms = 1.0 / rms
    normed = combined * inv_rms
    g = jnp.concatenate([gb[0], gb[1]], axis=1).astype(F32) * (gain_t * (1.0 - LAMBDA_INIT))
    grad = ((g - normed * jnp.mean(g * normed, axis=0, keepdims=True)) * inv_rms).astype(BF16)
    gt[...] = grad
    grad32 = grad.astype(F32)
    gn[...] = jnp.transpose(grad32).astype(BF16)
    stat1 = jnp.sum(grad32 * (ot[:, :256] * inv[0]), axis=0, keepdims=True)
    stat2 = jnp.sum(grad32 * (ot[:, 256:] * inv[1]), axis=0, keepdims=True)
    inv1 = inv[0]
    inv2 = inv[1] * lam_own

    dq[...] = jnp.zeros_like(dq)

    def backward(s, r):
        i = s * 2 + r
        dp = mm(vb[:, s, r].reshape(256, 256), gt[...])
        keys = kb[:, s, r].reshape(256, 256)
        p1 = jnp.concatenate([st[0, 0, i] * (inv1 * scales[0]), st[0, 1, i] * inv1], axis=0)
        p2 = jnp.concatenate([st[1, 0, i] * (inv2 * scales[1]), st[1, 1, i] * inv2], axis=0)
        mixed = (p1 - p2).astype(BF16)
        ds1 = (p1 * (dp - stat1)).astype(BF16)
        ds2 = (p2 * (dp - stat2)).astype(BF16)
        dv = mm(mixed, gn[...])
        dk1 = mm(ds1, qb[:, 0:128]) * SCALE
        dk2 = mm(ds2, qb[:, 128:256]) * -SCALE
        dq[0] += mm(keys[:, 0:128], ds1, TN)
        dq[1] += mm(keys[:, 128:256], ds2, TN)
        for part, at in ((dk1, 0), (dk2, 128), (dv, 256)):
            cols = pl.ds(at, part.shape[1])
            for t in range(2):
                piece = part[t * 128 : t * 128 + 128]
                if r:
                    sibs[s, t, :, cols] = piece.astype(BF16)
                else:
                    own[t, s, :, cols] = piece
        if r:
            send(sibs.at[s], sibr.at[s], ("sib", s), sib)

    left, right, both = pl.ds(0, 256), pl.ds(256, 256), pl.ds(0, 512)

    def total(t, s, cols):
        return own[t, s, :, cols] + sibr[s, t, :, cols].astype(F32)

    def chip_sum(t, s, cols):
        ys[t, s, :, cols] = total(t, s, cols).astype(BF16)

    def pass_on(t, s, cols, *key):
        send(ys.at[t, s, :, cols], yr.at[t, s, :, cols], ("yr", t, *key), ydev[s])

    def straight(t, s, cols, *key):
        chip_sum(t, s, cols)
        pass_on(t, s, cols, *key)

    all_sent()
    backward(2, 1)
    backward(2, 0)
    backward(1, 1)
    def halfway(t, up, down, *key, rows=pl.ds(0, 128)):
        send(ys.at[t, 2, rows, up], yr.at[t, 0, rows, up], ("halfway", t, *key), ydev[1])
        send(ys.at[t, 2, rows, down], yr.at[t, 0, rows, down], ("halfway", t, *key), ydev[3])

    def second_hop(t, up, down, n, rows=pl.ds(0, 128)):
        for s, cols in ((1, up), (3, down)):
            here = own[t, s, rows, cols] + sibr[s, t, rows, cols].astype(F32)
            ys[t, s, rows, cols] = (here + yr[t, 0, rows, cols].astype(F32)).astype(BF16)
            send(ys.at[t, s, rows, cols], yr.at[t, s, rows, cols], ("yr", t, n), ydev[s])

    groups = [(pl.ds(q * 128, 128), pl.ds(256 + q * 128, 128)) for q in range(2)]
    a_group = yr.at[1, 0, :, left]

    arrived(sibr.at[2], "sib", 2)
    chip_sum(1, 2, both)
    row_halves = [pl.ds(0, 64), pl.ds(64, 64)]
    for q, (up, down) in enumerate(groups):
        for h in range(2):
            halfway(1, up, down, q, h, rows=row_halves[h])
    backward(3, 1)
    backward(1, 0)
    arrived(sibr.at[1], "sib", 1)
    straight(1, 1, right, 2)
    backward(3, 0)
    arrived(sibr.at[3], "sib", 3)
    straight(1, 3, left, 2)
    chip_sum(0, 2, both)
    halfway(0, left, right)
    backward(0, 1)
    backward(0, 0)
    for j, sign in ((0, SCALE), (1, -SCALE)):
        rb[0, j * 128 : j * 128 + 128] = (dq[j, :, 0:128] * sign).astype(BF16)
        dqs[j * 128 : j * 128 + 128] = (dq[j, :, 128:256] * sign).astype(BF16)
    send(dqs, rb.at[0, pl.ds(256, 256)], ("dq",), far)
    for q, (up, down) in enumerate(groups):
        for h in range(2):
            arrived(yr.at[1, 0, row_halves[h], left], "halfway", 1, q, h)
            second_hop(1, up, down, q, row_halves[h])
    straight(0, 1, right, 0)
    straight(0, 3, left, 0)
    arrived(sibr.at[0], "sib", 0)

    def finish(t, cols):
        whole = total(t, 0, cols) + (yr[t, 1, :, cols].astype(F32) + yr[t, 3, :, cols].astype(F32))
        return jnp.transpose(whole).astype(BF16)

    arrived(yr.at[0, 0], "halfway", 0)
    second_hop(0, left, right, 0)
    arrived(yr.at[1, 0], "yr", 1, 2)
    for q, group in enumerate(groups):
        arrived(a_group, "yr", 1, q)
        for cols in group:
            dks[cols, :] = finish(1, cols)
            send(dks.at[cols], rb.at[2, cols], ("dk",), far)

    blocks = [(1, 2), (1, 1), (1, 3), (0, 2), (0, 1), (0, 3), (1, 0), (0, 0)]

    def rows(r, s):
        block = lax.rem(lo + r, 2) * 4 + lax.rem(x + s, 4)
        return pl.ds(pl.multiple_of(block * 512, 512), 512)

    loaded(wb, 5)
    arrived(rb.at[0, pl.ds(256, 256)], "dq")
    for r, s in blocks:
        pa[r, s] = mm(wb[0, rows(r, s)], rb[0])
    arrived(yr.at[0, pl.ds(0, 2)], "yr", 0, 0)
    for cols in (left, right):
        rb[1, cols, :] = finish(0, cols)
    early = blocks[:2]
    for r, s in early:
        pa[r, s] += mm(wb[1, rows(r, s)], rb[1])
    arrived(rb.at[2], "dk")

    def project(r, s):
        near = 0 if (r, s) in early else mm(wb[1, rows(r, s)], rb[1])
        return pa[r, s] + (near + mm(wb[2, rows(r, s)], rb[2]))

    pieces = (2, 4)

    def features(r, q):
        return pl.ds(q * (512 // pieces[r]), 512 // pieces[r])

    def top(r, q):
        return pl.ds(q * (512 // pieces[r]), 256 // pieces[r])

    def bottom(r, q):
        return pl.ds(q * (512 // pieces[r]) + 256 // pieces[r], 256 // pieces[r])

    def x_first(r):
        xs_[r, 2] = project(r, 2).astype(BF16)
        for q in range(pieces[r]):
            send(xs_.at[r, 2, top(r, q)], xr.at[r, top(r, q)], ("xr", r, q), xdev[1])
            send(xs_.at[r, 2, bottom(r, q)], xr.at[r, bottom(r, q)], ("xr", r, q), xdev[3])

    def x_pass(r, s, part, q):
        send(xs_.at[r, s, part], xf.at[r, s // 2, part], ("xf", r, q if r else 0), xdev[s])

    def x_direct(r):
        for q in range(pieces[r]):
            for s, part in ((1, bottom(r, q)), (3, top(r, q))):
                xs_[r, s, part] = pa[r, s, part].astype(BF16)
                x_pass(r, s, part, q)

    def x_second(r, q):
        arrived(xr.at[r, features(r, q)], "xr", r, q)
        for s, part in ((1, top(r, q)), (3, bottom(r, q))):
            xs_[r, s, part] = (pa[r, s, part] + xr[r, part].astype(F32)).astype(BF16)
            x_pass(r, s, part, q)

    x_first(1)
    pa[1, 1] = project(1, 1)
    pa[1, 3] = project(1, 3)
    x_direct(1)
    x_first(0)
    for r, s in ((0, 1), (0, 3), (1, 0), (0, 0)):
        pa[r, s] = project(r, s)
    for q in range(pieces[1]):
        x_second(1, q)
    x_direct(0)
    for q in range(pieces[0]):
        x_second(0, q)
    for q in range(pieces[1]):
        part = features(1, q)
        arrived(xf.at[1, :, part], "xf", 1, q)
        zs[part, :] = (pa[1, 0, part] + (xf[1, 0, part].astype(F32) + xf[1, 1, part].astype(F32))).astype(BF16)
        send(zs.at[part], zr.at[part], ("zr",), partner)
    arrived(xf.at[0], "xf", 0, 0)
    ob[...] = pa[0, 0] + (xf[0, 0].astype(F32) + xf[0, 1].astype(F32))
    done = load(ob, out, 6)
    all_sent()
    done.wait()
    arrived(zr, "zr")
    assert len(names) == RECEIVES, len(names)


def body(order, qh, kh, vh, og, wq, wk, wv, wo, lam, gain):
    any_ = pl.BlockSpec(memory_space=pl.ANY)
    v = pltpu.VMEM
    parts = pl.pallas_call(
        kernel,
        out_shape=(
            jax.ShapeDtypeStruct((512, 128), F32),
            jax.ShapeDtypeStruct((512, 128), BF16),
        ),
        in_specs=[any_] * 11,
        out_specs=(any_, any_),
        scratch_shapes=[
            pltpu.SMEM((32,), jnp.int32),
            pltpu.SMEM((2,), F32),
            v((1, 256), F32),
            v((2, 4, 2, 128, 256), BF16),
            v((2, 4, 2, 128, 256), BF16),
            v((256, 256), BF16),
            v((256, 128), BF16),
            v((2, 256, 128), BF16),
            v((2, 4, 128, 512), BF16),
            v((2, 4, 512, 512), BF16),
            v((3, 4096, 512), BF16),
            v((2, 2, 8, 128, 256), F32),
            v((2, 8, 128, 512), BF16),
            v((2, 128, 256), BF16),
            v((64, 256), jnp.int32),
            v((256, 512), F32),
            v((512, 128), F32),
            v((256, 256), BF16),
            v((256, 256), BF16),
            v((2, 128, 256), F32),
            v((4, 2, 128, 512), BF16),
            v((4, 2, 128, 512), BF16),
            v((2, 4, 128, 512), F32),
            v((2, 4, 128, 512), BF16),
            v((2, 4, 128, 512), BF16),
            v((256, 128), BF16),
            v((512, 128), BF16),
            v((3, 512, 128), BF16),
            v((2, 4, 512, 128), F32),
            v((2, 4, 512, 128), BF16),
            v((2, 512, 128), BF16),
            v((2, 2, 512, 128), BF16),
            v((512, 128), BF16),
            v((512, 128), F32),
            pltpu.SemaphoreType.DMA((LOADS,)),
            pltpu.SemaphoreType.DMA((1,)),
            pltpu.SemaphoreType.DMA((RECEIVES,)),
        ],
        compiler_params=pltpu.CompilerParams(
            collective_id=0, has_side_effects=True, vmem_limit_bytes=56 * 2**20
        ),
        name="differential_attention_backward",
    )(order, lam, gain.reshape(1, 256), qh, kh, vh, og, wq, wk, wv, wo)
    return parts[0] + parts[1].astype(F32)


def solution(mesh):
    in_specs = (
        P(),
        P("ctx", "heads"),
        P("ctx", "heads"),
        P("ctx", "heads"),
        P("ctx", "heads"),
        P(None, "heads"),
        P(None, "heads"),
        P(None, "heads"),
        P("heads", None),
        P("heads"),
        P(),
    )
    out_specs = P("heads", "ctx")
    return jax.shard_map(body, mesh=mesh, in_specs=in_specs, out_specs=out_specs, check_vma=False)
```
